512 devices in a mesh: bunch: 8 (over x, core), dom: 64 (over z, y).
Axes of the slice: x: 4, y: 8, z: 8, core: 2. Of those that a mesh axis runs over, the one named last changes fastest.
Arguments:
- coords: bfloat16 [512, 2, 32768], P('bunch', None, 'dom'), may hold values from -6 to 6
- slice_index: int32 [512, 32768], P('bunch', 'dom'), may hold values from 0 to 511
- history: float32 [512, 16, 2, 512], P('bunch'), may hold values from -6 to 6
- turn_coef: float32 [16, 2], replicated, may hold values from 0.02 to 0.2
- fill: int32 [512], replicated, may hold values from 0 to 1023, as said below
- panels: bfloat16 [2, 4, 512, 512], P(None, None, 'dom'), may hold values from -0.25 to 0.25
Outputs:
- particle_kick: bfloat16 [512, 2, 32768], P('bunch', None, 'dom')
The draws below stay inside these ranges and needn't reach their ends.
Inputs may be any that keep to these rules, and one draw needn't show every extreme that they name: fill rises strictly along the train; the first bunch sits in bucket 0 and the last in bucket 1024 - 1.
All inputs are finite; a program needn't handle non-finite values.
Results may differ from the reference program's by a relative error of at most 0.0049.
Values may be sent and summed in bfloat16 or wider, within the bound.
No kernel may reach another device: no remote copies, remote signals or barrier semaphores. Data moves between devices by JAX's collectives and lax.ppermute only.
A program may use at most 64 MiB of HBM per device.

```python
import math
import jax
import jax.numpy as jnp
from jax import lax

SLICES = 512
PANELS = 4
TURNS = 16
NB = 512
PARTICLES = 32768
CYCLE = 1024


def draw_fill(key, part):
    shuffled = jax.random.permutation(key, CYCLE - 2)[:NB - 2] + 1
    inner = jnp.sort(shuffled).astype(jnp.int32)
    first = jnp.zeros((1,), jnp.int32)
    last = jnp.full((1,), CYCLE - 1, jnp.int32)
    return jnp.concatenate([first, inner, last], 0)


def with_ends(array, stream_key, least, largest):
    longest = array.shape.index(max(array.shape))
    spots = []
    for shift in (0, 1):
        where = [jax.random.randint(jax.random.fold_in(stream_key, axis), (), 0, length) for axis, length in enumerate(array.shape)]
        where[longest] = (where[longest] + shift) % array.shape[longest]
        spots.append(tuple(where))
    return array.at[spots[0]].set(least).at[spots[1]].set(largest)


def shard_levels(own_key, shape, pieces, low, top_value):
    def one(position, blocks):
        heights = jax.random.uniform(jax.random.fold_in(jax.random.fold_in(own_key, 6), position), (blocks,), jnp.float32, low / len(pieces), top_value / len(pieces))
        return jnp.repeat(jnp.exp(heights), shape[position] // blocks).reshape((-1,) + (1,) * (len(shape) - position - 1))

    gain = one(*pieces[0])
    for cut in pieces[1:]:
        gain = gain * one(*cut)
    return gain


def normal_values(stream_key, extent, width, reach, shards=(), kind=jnp.bfloat16):
    array = jax.random.normal(stream_key, extent, jnp.float32) * width
    if len(shards) > 0:
        array = shard_levels(stream_key, extent, shards, -0.22, 0.18) * array
    return jnp.clip(array, min=-reach, max=reach).astype(kind)


def setup_inputs(seed: int = 0) -> dict:
    keys = jax.random.split(jax.random.key(seed), 7)
    coords = normal_values(keys[0], (NB, 2, PARTICLES), 1.0, 6.0, ((0, 8), (2, 64)))
    slice_index = with_ends(jax.random.randint(keys[1], (NB, PARTICLES), 0, SLICES), jax.random.fold_in(keys[1], 1), 0, SLICES - 1).astype(jnp.int32)
    history = normal_values(keys[2], (NB, TURNS, 2, SLICES), 1.0, 6.0, ((0, 8),), jnp.float32)
    turn_coef = jnp.clip(jnp.exp(jax.random.uniform(keys[3], (TURNS, 2), jnp.float32, math.log(0.02), math.log(0.2))), 0.02, 0.2)
    fill = draw_fill(jax.random.fold_in(keys[6], 71), 0)
    panels = normal_values(keys[5], (2, PANELS, SLICES, SLICES), SLICES ** -0.5, 0.25, ((2, 64),))
    return {"coords": coords, "slice_index": slice_index, "history": history, "turn_coef": turn_coef, "fill": fill, "panels": panels}


def reference(coords, slice_index, history, turn_coef, fill, panels):
    scale = (SLICES / PARTICLES) ** 0.5
    flat = (jnp.arange(NB, dtype=jnp.int32)[:, None] * SLICES + slice_index).reshape(-1)
    planes = []
    for plane in range(2):
        values = coords[:, plane, :].astype(jnp.float32).reshape(-1)
        summed = jax.ops.segment_sum(values, flat, num_segments=NB * SLICES)
        planes.append(summed.reshape(NB, SLICES))
    moment = jnp.stack(planes, 1) * scale
    carried = jnp.einsum("btps,tp->bps", history, turn_coef, precision=lax.Precision.HIGHEST)
    source = (moment + carried).astype(jnp.bfloat16)
    gaps = jnp.stack([jnp.mod(fill - jnp.roll(fill, offset), CYCLE) for offset in range(PANELS)], 0)
    shifted = jnp.stack([jnp.roll(source, offset, axis=0) for offset in range(PANELS)], 0)
    chosen = []
    for panel in range(PANELS):
        hits = (gaps == panel)[:, :, None, None]
        chosen.append(jnp.sum(jnp.where(hits, shifted, jnp.zeros((), jnp.bfloat16)), axis=0).astype(jnp.bfloat16))
    selected = jnp.stack(chosen, 0)
    kick = jnp.einsum("pksj,kbpj->bps", panels.astype(jnp.float32), selected.astype(jnp.float32),
                      precision=lax.Precision.HIGHEST).astype(jnp.bfloat16)
    lookup = jnp.broadcast_to(slice_index[:, None, :], (NB, 2, PARTICLES))
    return jnp.take_along_axis(kick, lookup, axis=2)
```

```python
import functools

import jax
import jax.numpy as jnp
from jax import lax
from jax.experimental import pallas as pl
from jax.experimental.pallas import tpu as pltpu
from jax.sharding import Mesh
from jax.sharding import PartitionSpec as P

F32 = jnp.float32
BF16 = jnp.bfloat16
LANES = 128
DOM = ("zq", "z0", "y")
ROW16 = ("z0", "y")
COL4 = ("zq",)
COL8 = ("zq", "z0")
VMEM = pl.BlockSpec(memory_space=pltpu.VMEM)
HBM = pl.BlockSpec(memory_space=pl.ANY)
PARAMS = pltpu.CompilerParams(vmem_limit_bytes=32 * 1024 * 1024)


def bunch_moment(coords_ref, index_ref, b):
    count = index_ref.shape[1]
    row = index_ref[pl.ds(b, 1), :]
    low = jnp.broadcast_to(row & (LANES - 1), (LANES, count))
    high = jnp.broadcast_to(row >> 7, (8, count))
    onehot = jnp.where(
        low == lax.broadcasted_iota(jnp.int32, (LANES, count), 0), 1.0, 0.0
    ).astype(BF16)
    planes = coords_ref[b].astype(F32)
    sub = lax.broadcasted_iota(jnp.int32, (8, count), 0)
    both = jnp.where(sub < 4, planes[0:1], planes[1:2])
    left = jnp.where(high == (sub & 3), both, 0.0).astype(BF16)
    return lax.dot_general(
        left, onehot, (((1,), (1,)), ((), ())), preferred_element_type=F32
    )


def halo_kernel(scale, coords_ref, index_ref, hist_ref, coef_ref, halo_ref, carried_ref, hist, rows, sem):
    dom = lax.axis_index(DOM)
    bunches = index_ref.shape[0]
    copy = pltpu.make_async_copy(hist_ref.at[dom], hist, sem)
    copy.start()
    for b in range(8):
        rows[pl.ds(8 * b, 8), :] = scale * bunch_moment(coords_ref, index_ref, bunches - 8 + b)
    copy.wait()
    total = jnp.zeros(hist.shape[1:], F32)
    for turn in range(hist.shape[0]):
        for_turn = jnp.concatenate(
            [jnp.full((1, 1), coef_ref[turn, 0]), jnp.full((1, 1), coef_ref[turn, 1])], 0
        )
        total = total + hist[turn] * for_turn
    for plane in range(2):
        for high in range(4):
            carried_ref[pl.ds(plane * 4 + high, 1), :] = total[
                plane : plane + 1, high * LANES : (high + 1) * LANES
            ]

    @pl.when(dom >= bunches - 8)
    def _():
        at = pl.ds(pl.multiple_of((dom - (bunches - 8)) * 8, 8), 8)
        rows[at, :] = rows[at, :] + carried_ref[...]

    for ph in range(8):
        halo_ref[ph] = rows[pl.ds(ph, 8, stride=8), :]


def moment_kernel(scale, coords_ref, index_ref, carried_ref, out_ref, rows):
    dom = lax.axis_index(DOM)
    bunches = index_ref.shape[0]

    def one(b, _):
        rows[pl.ds(pl.multiple_of(8 * b, 8), 8), :] = scale * bunch_moment(coords_ref, index_ref, b)
        return 0

    lax.fori_loop(0, bunches, one, 0, unroll=8)
    at = pl.ds(pl.multiple_of(dom * 8, 8), 8)
    rows[at, :] = rows[at, :] + carried_ref[...]
    for ph in range(8):
        for half in range(2):
            for tile in range(4):
                first = (half * 32 + tile * 8) * 8
                out_ref[ph * 2 + half, pl.ds(8 + tile * 8, 8), :] = rows[pl.ds(first + ph, 8, stride=8), :]
            if half == 1:
                out_ref[ph * 2 + half, pl.ds(0, 8), :] = jnp.zeros((8, LANES), F32)


def sum_kernel(in_ref, out_ref):
    total = in_ref[0]
    for part in range(1, in_ref.shape[0]):
        total = total + in_ref[part]
    for copy in range(out_ref.shape[0]):
        out_ref[copy] = total


def source_kernel(in_ref, out_ref):
    total = in_ref[0]
    for part in range(1, in_ref.shape[0]):
        total = total + in_ref[part]
    total = jnp.concatenate([total, jnp.zeros((8, LANES), F32)], 0).astype(BF16)
    for copy in range(out_ref.shape[0]):
        out_ref[copy] = total


def kick_kernel(total_bunches, in_ref, panels_ref, fill_ref, out_ref, source, bucket):
    bunches = 64
    first = lax.axis_index("bunch") * bunches
    sub = lax.broadcasted_iota(jnp.int32, (8, LANES), 0)
    for tile in range(9):
        column = jnp.zeros((8, LANES), jnp.int32)
        for row in range(8):
            place = first - 8 + tile * 8 + row + total_bunches
            place = jnp.where(place >= total_bunches, place - total_bunches, place)
            column = jnp.where(sub == row, fill_ref[place], column)
        bucket[pl.ds(tile * 8, 8), :] = column
    for ph in range(8):
        source[ph, pl.ds(0, 40), :] = in_ref[2 * ph].astype(F32)[0:40]
        source[ph, pl.ds(40, 32), :] = in_ref[2 * ph + 1].astype(F32)[8:40]
    cycle = 2 * total_bunches
    here = bucket[pl.ds(8, bunches), :]
    gaps = [None] + [(here - bucket[pl.ds(8 - d, bunches), :]) & (cycle - 1) for d in (1, 2, 3)]
    outs = []
    for plane in range(2):
        picked = [[], [], [], []]
        for high in range(4):
            ph = plane * 4 + high
            past = [source[ph, pl.ds(8 - d, bunches), :] for d in range(4)]
            picked[0].append(past[0].astype(BF16))
            for k in (1, 2, 3):
                value = jnp.zeros((bunches, LANES), F32)
                for d in range(1, k + 1):
                    value = jnp.where(gaps[d] == k, past[d], value)
                picked[k].append(value.astype(BF16))
        total = None
        for k in range(4):
            right = jnp.concatenate(picked[k], 1)
            left = jnp.concatenate([panels_ref[y, plane, k] for y in range(8)], 0).astype(BF16)
            part = lax.dot_general(left, right, (((1,), (1,)), ((), ())), preferred_element_type=F32)
            total = part if total is None else total + part
        outs.append(total)
    kick = jnp.concatenate(outs, 1).astype(BF16)
    for copy in range(out_ref.shape[0]):
        out_ref[copy] = kick


def lookup_kernel(kick_ref, index_ref, out_ref, table):
    bunches = index_ref.shape[0]
    for high in range(4):
        rows = jnp.concatenate([kick_ref[2 * high].astype(F32), kick_ref[2 * high + 1].astype(F32)], 0)
        table[high] = rows.T
    for block in range(bunches // 8):
        for tile in range(index_ref.shape[1] // LANES):
            index = index_ref[pl.ds(block * 8, 8), pl.ds(tile * LANES, LANES)]
            low = index & (LANES - 1)
            top = index >> 7
            found = []
            for plane in range(2):
                value = None
                for high in range(4):
                    row = table[high, pl.ds(plane * bunches + block * 8, 8), :]
                    got = jnp.take_along_axis(row, low, axis=1)
                    value = got if value is None else jnp.where(top == high, got, value)
                found.append(value)
            out_ref[pl.ds(block * 8, 8), :, pl.ds(tile * LANES, LANES)] = jnp.stack(found, 1).astype(BF16)


def call(kernel, out_shape, in_specs, scratch=(), out_specs=None):
    return pl.pallas_call(
        kernel,
        out_shape=out_shape,
        in_specs=in_specs,
        out_specs=VMEM if out_specs is None else out_specs,
        scratch_shapes=list(scratch),
        compiler_params=PARAMS,
    )


def exchange(value, axes):
    return lax.all_to_all(value, axes, 0, 0, tiled=True)


def local(coords, slice_index, history, turn_coef, fill, panels):
    bunches, _, count = coords.shape
    slices = panels.shape[3]
    turns = history.shape[1]
    scale = (slices / (count * lax.axis_size(DOM))) ** 0.5
    shape = jax.ShapeDtypeStruct
    smem = pl.BlockSpec(memory_space=pltpu.SMEM)

    gathered = lax.all_gather(panels.astype(F32), "y", axis=0, tiled=False)

    halo, carried = call(
        functools.partial(halo_kernel, scale),
        (shape((8, 8, LANES), F32), shape((8, LANES), F32)),
        [VMEM, VMEM, HBM, smem],
        [pltpu.VMEM((turns, 2, slices), F32), pltpu.VMEM((64, LANES), F32), pltpu.SemaphoreType.DMA],
        (VMEM, VMEM),
    )(coords, slice_index, history, turn_coef)
    ring = lax.axis_size("bunch")
    halo = lax.ppermute(halo, "bunch", [(i, (i + 1) % ring) for i in range(ring)])
    partial = call(
        functools.partial(moment_kernel, scale),
        shape((16, 40, LANES), F32),
        [VMEM, VMEM, VMEM],
        [pltpu.VMEM((bunches * 8, LANES), F32)],
    )(coords, slice_index, carried)
    partial = partial.reshape(8, 2, 40, LANES).at[:, 0, 0:8].set(halo).reshape(16, 40, LANES)
    part = exchange(partial, ROW16)
    part = call(sum_kernel, shape((4, 40, LANES), F32), [VMEM])(part)
    part = exchange(part, COL4)
    source = call(source_kernel, shape((16, 48, LANES), BF16), [VMEM])(part)
    source = exchange(source, ROW16)
    kick = call(
        functools.partial(kick_kernel, bunches * ring),
        shape((8, 64, LANES), BF16),
        [VMEM, VMEM, smem],
        [pltpu.VMEM((8, 72, LANES), F32), pltpu.VMEM((72, LANES), jnp.int32)],
    )(source, gathered, fill)
    kick = exchange(kick, COL8)
    return call(
        lookup_kernel,
        shape((bunches, 2, count), BF16),
        [VMEM, VMEM],
        [pltpu.VMEM((4, LANES, LANES), F32)],
    )(kick, slice_index)


def solution(mesh):
    fine = Mesh(mesh.devices.reshape(8, 4, 2, 8), ("bunch", "zq", "z0", "y"))
    return jax.shard_map(
        local,
        mesh=fine,
        in_specs=(
            P("bunch", None, DOM),
            P("bunch", DOM),
            P("bunch", None, None, None),
            P(),
            P(),
            P(None, None, DOM, None),
        ),
        out_specs=P("bunch", None, DOM),
        check_vma=False,
    )
```

```python
import functools

import jax
import jax.numpy as jnp
from jax import lax
from jax.experimental import pallas as pl
from jax.experimental.pallas import tpu as pltpu
from jax.sharding import Mesh
from jax.sharding import PartitionSpec as P

F32 = jnp.float32
BF16 = jnp.bfloat16
LANES = 128
DOM = ("zq", "z0", "y")
ROW16 = ("z0", "y")
COL4 = ("zq",)
VMEM = pl.BlockSpec(memory_space=pltpu.VMEM)
HBM = pl.BlockSpec(memory_space=pltpu.HBM)
WIDE = pltpu.CompilerParams(vmem_limit_bytes=60 * 1024 * 1024)
PARAMS = pltpu.CompilerParams(vmem_limit_bytes=32 * 1024 * 1024)


def bunch_moment(coords_ref, index_ref, b):
    count = index_ref.shape[1]
    row = index_ref[pl.ds(b, 1), :]
    low = jnp.broadcast_to(row & (LANES - 1), (LANES, count))
    high = jnp.broadcast_to(row >> 7, (8, count))
    onehot = jnp.where(
        low == lax.broadcasted_iota(jnp.int32, (LANES, count), 0), 1.0, 0.0
    ).astype(BF16)
    planes = coords_ref[b].astype(F32)
    sub = lax.broadcasted_iota(jnp.int32, (8, count), 0)
    both = jnp.where(sub < 4, planes[0:1], planes[1:2])
    left = jnp.where(high == (sub & 3), both, 0.0).astype(BF16)
    return lax.dot_general(
        left, onehot, (((1,), (1,)), ((), ())), preferred_element_type=F32
    )


def halo_kernel(
    scale, coords_hbm, index_hbm, hist_hbm, coef_ref, halo_ref, carried_ref, coords, index, hist, rows, sems
):
    dom = lax.axis_index(DOM)
    bunches = index_hbm.shape[0]
    last = pl.ds(bunches - 8, 8)
    copies = [
        pltpu.make_async_copy(index_hbm.at[last], index, sems.at[0]),
        pltpu.make_async_copy(coords_hbm.at[last], coords, sems.at[1]),
        pltpu.make_async_copy(hist_hbm.at[dom], hist, sems.at[2]),
    ]
    for copy in copies:
        copy.start()
    copies[0].wait()
    copies[1].wait()
    for b in range(8):
        rows[pl.ds(8 * b, 8), :] = scale * bunch_moment(coords, index, b)
    copies[2].wait()
    total = jnp.zeros(hist.shape[1:], F32)
    for turn in range(hist.shape[0]):
        for_turn = jnp.concatenate(
            [jnp.full((1, 1), coef_ref[0, turn]), jnp.full((1, 1), coef_ref[1, turn])], 0
        )
        total = total + hist[turn] * for_turn
    for plane in range(2):
        for high in range(4):
            carried_ref[pl.ds(plane * 4 + high, 1), :] = total[
                plane : plane + 1, high * LANES : (high + 1) * LANES
            ]

    @pl.when(dom >= bunches - 8)
    def _():
        at = pl.ds(pl.multiple_of((dom - (bunches - 8)) * 8, 8), 8)
        rows[at, :] = rows[at, :] + carried_ref[...]

    for ph in range(8):
        halo_ref[ph] = rows[pl.ds(ph, 8, stride=8), :]


def moment_kernel(scale, coords_ref, index_ref, carried_ref, out_ref, rows):
    dom = lax.axis_index(DOM)
    bunches = index_ref.shape[0]

    def one(b, _):
        rows[pl.ds(pl.multiple_of(8 * b, 8), 8), :] = scale * bunch_moment(coords_ref, index_ref, b)
        return 0

    lax.fori_loop(0, bunches, one, 0, unroll=8)
    at = pl.ds(pl.multiple_of(dom * 8, 8), 8)
    rows[at, :] = rows[at, :] + carried_ref[...]
    for ph in range(8):
        for half in range(2):
            for tile in range(4):
                first = (half * 32 + tile * 8) * 8
                out_ref[ph * 2 + half, pl.ds(8 + tile * 8, 8), :] = rows[pl.ds(first + ph, 8, stride=8), :]
            if half == 1:
                out_ref[ph * 2 + half, pl.ds(0, 8), :] = jnp.zeros((8, LANES), F32)


def sum_kernel(in_ref, out_ref):
    total = in_ref[0]
    for part in range(1, in_ref.shape[0]):
        total = total + in_ref[part]
    for copy in range(out_ref.shape[0]):
        out_ref[copy] = total


def source_kernel(in_ref, out_ref):
    total = in_ref[0]
    for part in range(1, in_ref.shape[0]):
        total = total + in_ref[part]
    total = jnp.concatenate([total, jnp.zeros((8, LANES), F32)], 0).astype(BF16)
    for copy in range(out_ref.shape[0]):
        out_ref[copy] = total


def kick_kernel(total_bunches, in_ref, panels_ref, fill_ref, out_ref, source, bucket):
    bunches = 64
    first = lax.axis_index("bunch") * bunches
    sub = lax.broadcasted_iota(jnp.int32, (8, LANES), 0)
    for tile in range(9):
        column = jnp.zeros((8, LANES), jnp.int32)
        for row in range(8):
            place = first - 8 + tile * 8 + row + total_bunches
            place = jnp.where(place >= total_bunches, place - total_bunches, place)
            column = jnp.where(sub == row, fill_ref[place], column)
        bucket[pl.ds(tile * 8, 8), :] = column
    for ph in range(8):
        source[ph, pl.ds(0, 40), :] = in_ref[2 * ph].astype(F32)[0:40]
        source[ph, pl.ds(40, 32), :] = in_ref[2 * ph + 1].astype(F32)[8:40]
    cycle = 2 * total_bunches
    here = bucket[pl.ds(8, bunches), :]
    gaps = [None] + [(here - bucket[pl.ds(8 - d, bunches), :]) & (cycle - 1) for d in (1, 2, 3)]
    outs = []
    for plane in range(2):
        picked = [[], [], [], []]
        for high in range(4):
            ph = plane * 4 + high
            past = [source[ph, pl.ds(8 - d, bunches), :] for d in range(4)]
            picked[0].append(past[0].astype(BF16))
            for k in (1, 2, 3):
                value = jnp.zeros((bunches, LANES), F32)
                for d in range(1, k + 1):
                    value = jnp.where(gaps[d] == k, past[d], value)
                picked[k].append(value.astype(BF16))
        total = None
        for k in range(4):
            right = jnp.concatenate(picked[k], 1)
            left = panels_ref[plane, k]
            part = lax.dot_general(left, right, (((1,), (1,)), ((), ())), preferred_element_type=F32)
            total = part if total is None else total + part
        outs.append(total)
    kick = jnp.concatenate(outs, 1).astype(BF16)
    for copy in range(out_ref.shape[0]):
        out_ref[copy] = kick


def lookup_kernel(kick_ref, index_ref, out_ref, table):
    bunches = index_ref.shape[0]
    for high in range(4):
        rows = jnp.concatenate([kick_ref[16 * high + part].astype(F32) for part in range(16)], 0)
        table[high] = rows.T
    for block in range(bunches // 8):
        for tile in range(index_ref.shape[1] // LANES):
            index = index_ref[pl.ds(block * 8, 8), pl.ds(tile * LANES, LANES)]
            low = index & (LANES - 1)
            top = index >> 7
            found = []
            for plane in range(2):
                value = None
                for high in range(4):
                    row = table[high, pl.ds(plane * bunches + block * 8, 8), :]
                    got = jnp.take_along_axis(row, low, axis=1)
                    value = got if value is None else jnp.where(top == high, got, value)
                found.append(value)
            out_ref[pl.ds(block * 8, 8), :, pl.ds(tile * LANES, LANES)] = jnp.stack(found, 1).astype(BF16)


def call(kernel, out_shape, in_specs, scratch=(), out_specs=None, params=PARAMS):
    return pl.pallas_call(
        kernel,
        out_shape=out_shape,
        in_specs=in_specs,
        out_specs=VMEM if out_specs is None else out_specs,
        scratch_shapes=list(scratch),
        compiler_params=params,
    )


def exchange(value, axes):
    return lax.all_to_all(value, axes, 0, 0, tiled=True)


def local(coords, slice_index, history, turn_coef, fill, panels):
    bunches, _, count = coords.shape
    slices = panels.shape[3]
    turns = history.shape[1]
    scale = (slices / (count * lax.axis_size(DOM))) ** 0.5
    shape = jax.ShapeDtypeStruct
    smem = pl.BlockSpec(memory_space=pltpu.SMEM)

    halo, carried = call(
        functools.partial(halo_kernel, scale),
        (shape((8, 8, LANES), F32), shape((8, LANES), F32)),
        [HBM, HBM, HBM, smem],
        [
            pltpu.VMEM((8, 2, count), BF16),
            pltpu.VMEM((8, count), jnp.int32),
            pltpu.VMEM((turns, 2, slices), F32),
            pltpu.VMEM((64, LANES), F32),
            pltpu.SemaphoreType.DMA((3,)),
        ],
        (VMEM, VMEM),
        WIDE,
    )(coords, slice_index, history, turn_coef.T)
    ring = lax.axis_size("bunch")
    halo = lax.ppermute(halo, "bunch", [(i, (i + 1) % ring) for i in range(ring)])
    partial = call(
        functools.partial(moment_kernel, scale),
        shape((16, 40, LANES), F32),
        [VMEM, VMEM, VMEM],
        [pltpu.VMEM((bunches * 8, LANES), F32)],
    )(coords, slice_index, carried)
    partial = partial.reshape(8, 2, 40, LANES).at[:, 0, 0:8].set(halo).reshape(16, 40, LANES)
    part = exchange(partial, ROW16)
    part = call(sum_kernel, shape((4, 40, LANES), F32), [VMEM])(part)
    part = exchange(part, COL4)
    source = call(source_kernel, shape((16, 48, LANES), BF16), [VMEM])(part)
    source = exchange(source, ROW16)
    kick = call(
        functools.partial(kick_kernel, bunches * ring),
        shape((64, 8, LANES), BF16),
        [VMEM, VMEM, smem],
        [pltpu.VMEM((8, 72, LANES), F32), pltpu.VMEM((72, LANES), jnp.int32)],
    )(source, panels, fill)
    kick = exchange(kick, DOM)
    return call(
        lookup_kernel,
        shape((bunches, 2, count), BF16),
        [VMEM, VMEM],
        [pltpu.VMEM((4, LANES, LANES), F32)],
    )(kick, slice_index)


def solution(mesh):
    fine = Mesh(mesh.devices.reshape(8, 4, 2, 8), ("bunch", "zq", "z0", "y"))
    return jax.shard_map(
        local,
        mesh=fine,
        in_specs=(
            P("bunch", None, DOM),
            P("bunch", DOM),
            P("bunch", None, None, None),
            P(),
            P(),
            P(None, None, DOM, None),
        ),
        out_specs=P("bunch", None, DOM),
        check_vma=False,
    )
```

```python
import functools

import jax
import jax.numpy as jnp
from jax import lax
from jax.experimental import pallas as pl
from jax.experimental.pallas import tpu as pltpu
from jax.sharding import Mesh
from jax.sharding import PartitionSpec as P

F32 = jnp.float32
BF16 = jnp.bfloat16
LANES = 128
DOM = ("zq", "z0", "y")
ROW16 = ("z0", "y")
COL4 = ("zq",)
VMEM = pl.BlockSpec(memory_space=pltpu.VMEM)
HBM = pl.BlockSpec(memory_space=pltpu.HBM)
PARAMS = pltpu.CompilerParams(vmem_limit_bytes=32 * 1024 * 1024)


def lane_ids(count):
    return lax.broadcasted_iota(jnp.int32, (LANES, count), 0).astype(F32).astype(BF16)


def bunch_moment(coords_ref, index_ref, b, ids):
    count = index_ref.shape[1]
    row = index_ref[pl.ds(b, 1), :]
    low = jnp.broadcast_to((row & (LANES - 1)).astype(F32).astype(BF16), (LANES, count))
    onehot = jnp.where(low == ids, jnp.ones((), BF16), jnp.zeros((), BF16))
    high = jnp.broadcast_to(row >> 7, (8, count))
    planes = coords_ref[b].astype(F32)
    sub = lax.broadcasted_iota(jnp.int32, (8, count), 0)
    both = jnp.where(sub < 4, planes[0:1], planes[1:2])
    left = jnp.where(high == (sub & 3), both, 0.0).astype(BF16)
    return lax.dot_general(
        left, onehot, (((1,), (1,)), ((), ())), preferred_element_type=F32
    )


def add_past_turns(hist, coef_ref, rows, first):
    plane_ids = lax.broadcasted_iota(jnp.int32, hist.shape[1:], 0)
    total = jnp.zeros(hist.shape[1:], F32)
    for turn in range(hist.shape[0]):
        total = total + hist[turn] * jnp.where(plane_ids == 0, coef_ref[0, turn], coef_ref[1, turn])
    parts = [
        total[plane : plane + 1, high * LANES : (high + 1) * LANES]
        for plane in range(2)
        for high in range(4)
    ]
    at = pl.ds(pl.multiple_of(first, 8), 8)
    rows[at, :] = rows[at, :] + jnp.concatenate(parts, 0)


def halo_kernel(
    scale, coords_hbm, index_hbm, hist_hbm, coef_hbm, halo_ref, coords, index, hist, coef_ref, rows, sems
):
    dom = lax.axis_index(DOM)
    bunches = index_hbm.shape[0]
    last = pl.ds(bunches - 8, 8)
    copy_index = pltpu.make_async_copy(index_hbm.at[last], index, sems.at[0])
    copy_coords = pltpu.make_async_copy(coords_hbm.at[last], coords, sems.at[1])
    copy_hist = pltpu.make_async_copy(hist_hbm.at[dom], hist, sems.at[2])
    copy_coef = pltpu.make_async_copy(coef_hbm, coef_ref, sems.at[3])
    copy_index.start()
    copy_coords.start()
    copy_hist.start()
    copy_coef.start()
    copy_index.wait()
    copy_coords.wait()
    ids = lane_ids(index.shape[1])
    for b in range(8):
        rows[pl.ds(8 * b, 8), :] = scale * bunch_moment(coords, index, b, ids)
    copy_hist.wait()
    copy_coef.wait()

    @pl.when(dom >= bunches - 8)
    def _():
        add_past_turns(hist, coef_ref, rows, (dom - (bunches - 8)) * 8)

    for ph in range(8):
        halo_ref[ph] = rows[pl.ds(ph, 8, stride=8), :]


def moment_kernel(scale, coords_ref, index_ref, hist_hbm, coef_hbm, out_ref, hist, coef_ref, rows, sems):
    dom = lax.axis_index(DOM)
    bunches = index_ref.shape[0]
    copy_hist = pltpu.make_async_copy(hist_hbm.at[dom], hist, sems.at[0])
    copy_coef = pltpu.make_async_copy(coef_hbm, coef_ref, sems.at[1])
    copy_hist.start()
    copy_coef.start()
    ids = lane_ids(index_ref.shape[1])

    def one(b, _):
        rows[pl.ds(pl.multiple_of(8 * b, 8), 8), :] = scale * bunch_moment(coords_ref, index_ref, b, ids)
        return 0

    lax.fori_loop(0, bunches, one, 0, unroll=8)
    copy_hist.wait()
    copy_coef.wait()
    add_past_turns(hist, coef_ref, rows, dom * 8)
    for ph in range(8):
        for half in range(2):
            for tile in range(4):
                first = (half * 32 + tile * 8) * 8
                out_ref[ph * 2 + half, pl.ds(8 + tile * 8, 8), :] = rows[pl.ds(first + ph, 8, stride=8), :]
            if half == 1:
                out_ref[ph * 2 + half, pl.ds(0, 8), :] = jnp.zeros((8, LANES), F32)


def sum_kernel(in_ref, out_ref):
    total = in_ref[0]
    for part in range(1, in_ref.shape[0]):
        total = total + in_ref[part]
    for copy in range(out_ref.shape[0]):
        out_ref[copy] = total


def source_kernel(in_ref, out_ref):
    total = in_ref[0]
    for part in range(1, in_ref.shape[0]):
        total = total + in_ref[part]
    total = jnp.concatenate([total, jnp.zeros((8, LANES), F32)], 0).astype(BF16)
    for copy in range(out_ref.shape[0]):
        out_ref[copy] = total


def kick_kernel(total_bunches, in_ref, panels_ref, fill_ref, out_ref, source, bucket):
    bunches = 64
    first = lax.axis_index("bunch") * bunches
    sub = lax.broadcasted_iota(jnp.int32, (8, LANES), 0)
    for tile in range(9):
        column = jnp.zeros((8, LANES), jnp.int32)
        for row in range(8):
            place = first - 8 + tile * 8 + row + total_bunches
            place = jnp.where(place >= total_bunches, place - total_bunches, place)
            column = jnp.where(sub == row, fill_ref[place], column)
        bucket[pl.ds(tile * 8, 8), :] = column
    for ph in range(8):
        source[ph, pl.ds(0, 40), :] = in_ref[2 * ph].astype(F32)[0:40]
        source[ph, pl.ds(40, 32), :] = in_ref[2 * ph + 1].astype(F32)[8:40]
    cycle = 2 * total_bunches
    here = bucket[pl.ds(8, bunches), :]
    gaps = [None] + [(here - bucket[pl.ds(8 - d, bunches), :]) & (cycle - 1) for d in (1, 2, 3)]
    outs = []
    for plane in range(2):
        picked = [[], [], [], []]
        for high in range(4):
            ph = plane * 4 + high
            past = [source[ph, pl.ds(8 - d, bunches), :] for d in range(4)]
            picked[0].append(past[0].astype(BF16))
            for k in (1, 2, 3):
                value = jnp.zeros((bunches, LANES), F32)
                for d in range(1, k + 1):
                    value = jnp.where(gaps[d] == k, past[d], value)
                picked[k].append(value.astype(BF16))
        total = None
        for k in range(4):
            right = jnp.concatenate(picked[k], 1)
            left = panels_ref[plane, k]
            part = lax.dot_general(left, right, (((1,), (1,)), ((), ())), preferred_element_type=F32)
            total = part if total is None else total + part
        outs.append(total)
    kick = jnp.concatenate(outs, 1).astype(BF16)
    for copy in range(out_ref.shape[0]):
        out_ref[copy] = kick


def lookup_kernel(kick_ref, index_ref, out_ref, table):
    bunches = index_ref.shape[0]
    for high in range(4):
        rows = jnp.concatenate([kick_ref[16 * high + part].astype(F32) for part in range(16)], 0)
        table[high] = rows.T
    for block in range(bunches // 8):
        for tile in range(index_ref.shape[1] // LANES):
            index = index_ref[pl.ds(block * 8, 8), pl.ds(tile * LANES, LANES)]
            low = index & (LANES - 1)
            top = index >> 7
            found = []
            for plane in range(2):
                value = None
                for high in range(4):
                    row = table[high, pl.ds(plane * bunches + block * 8, 8), :]
                    got = jnp.take_along_axis(row, low, axis=1)
                    value = got if value is None else jnp.where(top == high, got, value)
                found.append(value)
            out_ref[pl.ds(block * 8, 8), :, pl.ds(tile * LANES, LANES)] = jnp.stack(found, 1).astype(BF16)


def call(kernel, out_shape, in_specs, scratch=()):
    return pl.pallas_call(
        kernel,
        out_shape=out_shape,
        in_specs=in_specs,
        out_specs=VMEM,
        scratch_shapes=list(scratch),
        compiler_params=PARAMS,
    )


def exchange(value, axes):
    return lax.all_to_all(value, axes, 0, 0, tiled=True)


def local(coords, slice_index, history, turn_coef, fill, panels):
    bunches, _, count = coords.shape
    slices = panels.shape[3]
    turns = history.shape[1]
    scale = (slices / (count * lax.axis_size(DOM))) ** 0.5
    shape = jax.ShapeDtypeStruct
    smem = pl.BlockSpec(memory_space=pltpu.SMEM)

    far = pltpu.with_memory_space_constraint
    coef = far(turn_coef.T, pltpu.HBM)
    past = far(history, pltpu.HBM)
    halo = call(
        functools.partial(halo_kernel, scale),
        pltpu.VMEM((8, 8, LANES), F32),
        [HBM, HBM, HBM, HBM],
        [
            pltpu.VMEM((8, 2, count), BF16),
            pltpu.VMEM((8, count), jnp.int32),
            pltpu.VMEM((turns, 2, slices), F32),
            pltpu.SMEM((2, turns), F32),
            pltpu.VMEM((64, LANES), F32),
            pltpu.SemaphoreType.DMA((4,)),
        ],
    )(far(coords, pltpu.HBM), far(slice_index, pltpu.HBM), past, coef)
    ring = lax.axis_size("bunch")
    halo = lax.ppermute(halo, "bunch", [(i, (i + 1) % ring) for i in range(ring)])
    partial = call(
        functools.partial(moment_kernel, scale),
        shape((16, 40, LANES), F32),
        [VMEM, VMEM, HBM, HBM],
        [
            pltpu.VMEM((turns, 2, slices), F32),
            pltpu.SMEM((2, turns), F32),
            pltpu.VMEM((bunches * 8, LANES), F32),
            pltpu.SemaphoreType.DMA((2,)),
        ],
    )(coords, slice_index, past, coef)
    partial = partial.reshape(8, 2, 40, LANES).at[:, 0, 0:8].set(halo).reshape(16, 40, LANES)
    part = exchange(partial, ROW16)
    part = call(sum_kernel, shape((4, 40, LANES), F32), [VMEM])(part)
    part = exchange(part, COL4)
    source = call(source_kernel, shape((16, 48, LANES), BF16), [VMEM])(part)
    source = exchange(source, ROW16)
    kick = call(
        functools.partial(kick_kernel, bunches * ring),
        shape((64, 8, LANES), BF16),
        [VMEM, VMEM, smem],
        [pltpu.VMEM((8, 72, LANES), F32), pltpu.VMEM((72, LANES), jnp.int32)],
    )(source, panels, fill)
    kick = exchange(kick, DOM)
    return call(
        lookup_kernel,
        shape((bunches, 2, count), BF16),
        [VMEM, VMEM],
        [pltpu.VMEM((4, LANES, LANES), F32)],
    )(kick, slice_index)


def solution(mesh):
    fine = Mesh(mesh.devices.reshape(8, 4, 2, 8), ("bunch", "zq", "z0", "y"))
    return jax.shard_map(
        local,
        mesh=fine,
        in_specs=(
            P("bunch", None, DOM),
            P("bunch", DOM),
            P("bunch", None, None, None),
            P(),
            P(),
            P(None, None, DOM, None),
        ),
        out_specs=P("bunch", None, DOM),
        check_vma=False,
    )
```

```python
import functools

import jax
import jax.numpy as jnp
from jax import lax
from jax.experimental import pallas as pl
from jax.experimental.pallas import tpu as pltpu
from jax.sharding import Mesh
from jax.sharding import PartitionSpec as P

F32 = jnp.float32
BF16 = jnp.bfloat16
LANES = 128
DOM = ("zq", "z0", "y")
ROW16 = ("z0", "y")
COL8 = ("zq", "z0")
VMEM = pl.BlockSpec(memory_space=pltpu.VMEM)
HBM = pl.BlockSpec(memory_space=pltpu.HBM)
PARAMS = pltpu.CompilerParams(vmem_limit_bytes=32 * 1024 * 1024)


def lane_ids(count):
    return lax.broadcasted_iota(jnp.int32, (LANES, count), 0).astype(F32).astype(BF16)


def bunch_moment(coords_ref, index_ref, b, ids):
    count = index_ref.shape[1]
    row = index_ref[pl.ds(b, 1), :]
    low = jnp.broadcast_to((row & (LANES - 1)).astype(F32).astype(BF16), (LANES, count))
    onehot = jnp.where(low == ids, jnp.ones((), BF16), jnp.zeros((), BF16))
    high = jnp.broadcast_to(row >> 7, (8, count))
    planes = coords_ref[b].astype(F32)
    sub = lax.broadcasted_iota(jnp.int32, (8, count), 0)
    both = jnp.where(sub < 4, planes[0:1], planes[1:2])
    left = jnp.where(high == (sub & 3), both, 0.0).astype(BF16)
    return lax.dot_general(
        left, onehot, (((1,), (1,)), ((), ())), preferred_element_type=F32
    )


def add_past_turns(hist, coef_ref, rows, first):
    plane_ids = lax.broadcasted_iota(jnp.int32, hist.shape[1:], 0)
    total = jnp.zeros(hist.shape[1:], F32)
    for turn in range(hist.shape[0]):
        total = total + hist[turn] * jnp.where(plane_ids == 0, coef_ref[0, turn], coef_ref[1, turn])
    parts = [
        total[plane : plane + 1, high * LANES : (high + 1) * LANES]
        for plane in range(2)
        for high in range(4)
    ]
    at = pl.ds(pl.multiple_of(first, 8), 8)
    rows[at, :] = rows[at, :] + jnp.concatenate(parts, 0)


def halo_kernel(
    scale, coords_hbm, index_hbm, hist_hbm, coef_hbm, halo_ref, coords, index, hist, coef_ref, rows, sems
):
    dom = lax.axis_index(DOM)
    bunches = index_hbm.shape[0]
    last = pl.ds(bunches - 8, 8)
    copy_index = pltpu.make_async_copy(index_hbm.at[last], index, sems.at[0])
    copy_coords = pltpu.make_async_copy(coords_hbm.at[last], coords, sems.at[1])
    copy_hist = pltpu.make_async_copy(hist_hbm.at[dom], hist, sems.at[2])
    copy_coef = pltpu.make_async_copy(coef_hbm, coef_ref, sems.at[3])
    copy_index.start()
    copy_coords.start()
    copy_hist.start()
    copy_coef.start()
    copy_index.wait()
    copy_coords.wait()
    ids = lane_ids(index.shape[1])
    for b in range(8):
        rows[pl.ds(8 * b, 8), :] = scale * bunch_moment(coords, index, b, ids)
    copy_hist.wait()
    copy_coef.wait()

    @pl.when(dom >= bunches - 8)
    def _():
        add_past_turns(hist, coef_ref, rows, (dom - (bunches - 8)) * 8)

    for ph in range(8):
        halo_ref[ph // 4, pl.ds((ph % 4) * 4, 4), :] = rows[pl.ds(32 + ph, 4, stride=8), :]


def moment_kernel(scale, coords_ref, index_ref, hist_hbm, coef_hbm, out_ref, hist, coef_ref, rows, sems):
    dom = lax.axis_index(DOM)
    bunches = index_ref.shape[0]
    copy_hist = pltpu.make_async_copy(hist_hbm.at[dom], hist, sems.at[0])
    copy_coef = pltpu.make_async_copy(coef_hbm, coef_ref, sems.at[1])
    copy_hist.start()
    copy_coef.start()
    ids = lane_ids(index_ref.shape[1])

    def one(b, _):
        rows[pl.ds(pl.multiple_of(8 * b, 8), 8), :] = scale * bunch_moment(coords_ref, index_ref, b, ids)
        return 0

    lax.fori_loop(0, bunches, one, 0, unroll=8)
    copy_hist.wait()
    copy_coef.wait()
    add_past_turns(hist, coef_ref, rows, dom * 8)
    for group in range(8):
        for ph in range(8):
            chunk, high = (ph // 4) * 8 + group, ph % 4
            if group > 0:
                out_ref[chunk, pl.ds(high * 4, 4), :] = rows[pl.ds((group * 8 - 4) * 8 + ph, 4, stride=8), :]
            out_ref[chunk, pl.ds(16 + high * 8, 8), :] = rows[pl.ds(group * 64 + ph, 8, stride=8), :]


def pair_kernel(bit, mine_ref, got_ref, both_ref):
    place_panels(bit, mine_ref, got_ref, both_ref)


def place_panels(bit, mine_ref, got_ref, both_ref):
    upper = (lax.axis_index("y") >> bit) & 1
    both_ref[upper] = mine_ref[...]
    both_ref[1 - upper] = got_ref[...]


def sum_kernel(in_ref, out_ref):
    total = in_ref[0]
    for part in range(1, in_ref.shape[0]):
        total = total + in_ref[part]
    for copy in range(out_ref.shape[0]):
        out_ref[copy] = total


def kick_kernel(total_bunches, bit, in_ref, mine_ref, got_ref, fill_ref, out_ref, source, bucket, wide):
    first = lax.axis_index("bunch") * 64 + lax.axis_index("y") * 8 - 4 + total_bunches
    sub = lax.broadcasted_iota(jnp.int32, (8, LANES), 0)
    for tile in range(2):
        column = jnp.zeros((8, LANES), jnp.int32)
        for row in range(8 if tile == 0 else 4):
            place = first + tile * 8 + row
            place = jnp.where(place >= total_bunches, place - total_bunches, place)
            column = jnp.where(sub == row, fill_ref[place], column)
        bucket[pl.ds(tile * 8, 8), :] = column
    place_panels(bit, mine_ref, got_ref, wide)
    for plane in range(2):
        total = in_ref[plane]
        for part in range(1, in_ref.shape[0] // 2):
            total = total + in_ref[2 * part + plane]
        total = total.astype(BF16).astype(F32)
        for high in range(4):
            source[plane, high, pl.ds(4, 4), :] = total[high * 4 : high * 4 + 4]
            source[plane, high, pl.ds(8, 8), :] = total[16 + high * 8 : 24 + high * 8]
    cycle = 2 * total_bunches
    here = bucket[pl.ds(4, 8), :]
    gaps = [None] + [(here - bucket[pl.ds(4 - d, 8), :]) & (cycle - 1) for d in (1, 2, 3)]
    outs = []
    for plane in range(2):
        picked = [[], [], [], []]
        for high in range(4):
            past = [source[plane, high, pl.ds(8 - d, 8), :] for d in range(4)]
            picked[0].append(past[0])
            for k in (1, 2, 3):
                value = jnp.zeros((8, LANES), F32)
                for d in range(1, k + 1):
                    value = jnp.where(gaps[d] == k, past[d], value)
                picked[k].append(value)
        total = None
        for k in range(4):
            left = jnp.concatenate(picked[k], 1).astype(BF16)
            right = jnp.concatenate(
                [wide[y // 4, (y // 2) % 2, y % 2, plane, k].astype(F32) for y in range(8)], 0
            ).astype(BF16)
            part = lax.dot_general(left, right, (((1,), (1,)), ((), ())), preferred_element_type=F32)
            total = part if total is None else total + part
        outs.append(total)
    kick = jnp.concatenate(outs, 1).astype(BF16)
    for copy in range(out_ref.shape[0]):
        out_ref[copy] = kick


def lookup_kernel(kick_ref, index_ref, out_ref):
    bunches = index_ref.shape[0]
    half = LANES // 2
    lower = lax.broadcasted_iota(jnp.int32, (8, LANES), 1) < half
    for block in range(bunches // 8):
        table = [[], []]
        for high in range(4):
            first = kick_ref[2 * high * 8 + block].astype(F32)
            second = kick_ref[(2 * high + 1) * 8 + block].astype(F32)
            table[0].append(jnp.where(lower, first, pltpu.roll(second, half, 1)))
            table[1].append(jnp.where(lower, pltpu.roll(first, half, 1), second))
        for tile in range(index_ref.shape[1] // LANES):
            index = index_ref[pl.ds(block * 8, 8), pl.ds(tile * LANES, LANES)]
            low = index & (LANES - 1)
            top = index >> 7
            found = []
            for plane in range(2):
                value = None
                for high in range(4):
                    got = jnp.take_along_axis(table[plane][high], low, axis=1)
                    value = got if value is None else jnp.where(top == high, got, value)
                found.append(value)
            out_ref[pl.ds(block * 8, 8), :, pl.ds(tile * LANES, LANES)] = jnp.stack(found, 1).astype(BF16)


def call(kernel, out_shape, in_specs, scratch=()):
    return pl.pallas_call(
        kernel,
        out_shape=out_shape,
        in_specs=in_specs,
        out_specs=VMEM,
        scratch_shapes=list(scratch),
        compiler_params=PARAMS,
    )


def neighbour(value, bit):
    return lax.ppermute(value, "y", [(i, i ^ (1 << bit)) for i in range(8)])


def beside(bit, mine, got):
    return call(
        functools.partial(pair_kernel, bit),
        jax.ShapeDtypeStruct((2, *mine.shape), BF16),
        [VMEM, VMEM],
    )(mine, got)


def exchange(value, axes):
    return lax.all_to_all(value, axes, 0, 0, tiled=True)


def local(coords, slice_index, history, turn_coef, fill, panels):
    bunches, _, count = coords.shape
    slices = panels.shape[3]
    turns = history.shape[1]
    scale = (slices / (count * lax.axis_size(DOM))) ** 0.5
    shape = jax.ShapeDtypeStruct
    smem = pl.BlockSpec(memory_space=pltpu.SMEM)

    far = pltpu.with_memory_space_constraint
    coef = far(turn_coef.T, pltpu.HBM)
    past = far(history, pltpu.HBM)
    halo = call(
        functools.partial(halo_kernel, scale),
        pltpu.VMEM((2, 16, LANES), F32),
        [HBM, HBM, HBM, HBM],
        [
            pltpu.VMEM((8, 2, count), BF16),
            pltpu.VMEM((8, count), jnp.int32),
            pltpu.VMEM((turns, 2, slices), F32),
            pltpu.SMEM((2, turns), F32),
            pltpu.VMEM((64, LANES), F32),
            pltpu.SemaphoreType.DMA((4,)),
        ],
    )(far(coords, pltpu.HBM), far(slice_index, pltpu.HBM), past, coef)
    ring = lax.axis_size("bunch")
    halo = lax.ppermute(halo, "bunch", [(i, (i + 1) % ring) for i in range(ring)])
    got = neighbour(panels, 0)
    partial = call(
        functools.partial(moment_kernel, scale),
        shape((16, 48, LANES), F32),
        [VMEM, VMEM, HBM, HBM],
        [
            pltpu.VMEM((turns, 2, slices), F32),
            pltpu.SMEM((2, turns), F32),
            pltpu.VMEM((bunches * 8, LANES), F32),
            pltpu.SemaphoreType.DMA((2,)),
        ],
    )(coords, slice_index, past, coef)
    partial = partial.reshape(2, 8, 48, LANES).at[:, 0, 0:16].set(halo).reshape(16, 48, LANES)
    part = exchange(partial, ROW16)
    pair = beside(0, panels, got)
    four = beside(1, pair, neighbour(pair, 1))
    part = call(sum_kernel, shape((8, 48, LANES), F32), [VMEM])(part)
    got = neighbour(four, 2)
    part = exchange(part, COL8)
    kick = call(
        functools.partial(kick_kernel, bunches * ring, 2),
        shape((64, 8, LANES), BF16),
        [VMEM, VMEM, VMEM, smem],
        [
            pltpu.VMEM((2, 4, 16, LANES), F32),
            pltpu.VMEM((16, LANES), jnp.int32),
            pltpu.VMEM((2, *four.shape), BF16),
        ],
    )(part, four, got, fill)
    kick = exchange(kick, DOM)
    return call(lookup_kernel, shape((bunches, 2, count), BF16), [VMEM, VMEM])(kick, slice_index)


def solution(mesh):
    fine = Mesh(mesh.devices.reshape(8, 4, 2, 8), ("bunch", "zq", "z0", "y"))
    return jax.shard_map(
        local,
        mesh=fine,
        in_specs=(
            P("bunch", None, DOM),
            P("bunch", DOM),
            P("bunch", None, None, None),
            P(),
            P(),
            P(None, None, DOM, None),
        ),
        out_specs=P("bunch", None, DOM),
        check_vma=False,
    )
```

```python
import functools

import jax
import jax.numpy as jnp
from jax import lax
from jax.experimental import pallas as pl
from jax.experimental.pallas import tpu as pltpu
from jax.sharding import Mesh
from jax.sharding import PartitionSpec as P

F32 = jnp.float32
BF16 = jnp.bfloat16
LANES = 128
DOM = ("zq", "z0", "y")
ROW16 = ("z0", "y")
COL4 = ("zq",)
VMEM = pl.BlockSpec(memory_space=pltpu.VMEM)
HBM = pl.BlockSpec(memory_space=pltpu.HBM)
PARAMS = pltpu.CompilerParams(vmem_limit_bytes=32 * 1024 * 1024)


def lane_ids(count):
    return lax.broadcasted_iota(jnp.int32, (LANES, count), 0).astype(F32).astype(BF16)


def bunch_moment(coords_ref, index_ref, b, ids):
    count = index_ref.shape[1]
    row = index_ref[pl.ds(b, 1), :]
    low = jnp.broadcast_to((row & (LANES - 1)).astype(F32).astype(BF16), (LANES, count))
    onehot = jnp.where(low == ids, jnp.ones((), BF16), jnp.zeros((), BF16))
    high = jnp.broadcast_to(row >> 7, (8, count))
    planes = coords_ref[b].astype(F32)
    sub = lax.broadcasted_iota(jnp.int32, (8, count), 0)
    both = jnp.where(sub < 4, planes[0:1], planes[1:2])
    left = jnp.where(high == (sub & 3), both, 0.0).astype(BF16)
    return lax.dot_general(
        left, onehot, (((1,), (1,)), ((), ())), preferred_element_type=F32
    )


def add_past_turns(hist, coef_ref, rows, first):
    plane_ids = lax.broadcasted_iota(jnp.int32, hist.shape[1:], 0)
    total = jnp.zeros(hist.shape[1:], F32)
    for turn in range(hist.shape[0]):
        total = total + hist[turn] * jnp.where(plane_ids == 0, coef_ref[0, turn], coef_ref[1, turn])
    parts = [
        total[plane : plane + 1, high * LANES : (high + 1) * LANES]
        for plane in range(2)
        for high in range(4)
    ]
    at = pl.ds(pl.multiple_of(first, 8), 8)
    rows[at, :] = rows[at, :] + jnp.concatenate(parts, 0)


def halo_kernel(
    scale, coords_hbm, index_hbm, hist_hbm, coef_hbm, halo_ref, coords, index, hist, coef_ref, rows, sems
):
    dom = lax.axis_index(DOM)
    bunches = index_hbm.shape[0]
    last = pl.ds(bunches - 8, 8)
    copy_index = pltpu.make_async_copy(index_hbm.at[last], index, sems.at[0])
    copy_coords = pltpu.make_async_copy(coords_hbm.at[last], coords, sems.at[1])
    copy_hist = pltpu.make_async_copy(hist_hbm.at[dom], hist, sems.at[2])
    copy_coef = pltpu.make_async_copy(coef_hbm, coef_ref, sems.at[3])
    copy_index.start()
    copy_coords.start()
    copy_hist.start()
    copy_coef.start()
    copy_index.wait()
    copy_coords.wait()
    ids = lane_ids(index.shape[1])
    for b in range(8):
        rows[pl.ds(8 * b, 8), :] = scale * bunch_moment(coords, index, b, ids)
    copy_hist.wait()
    copy_coef.wait()

    @pl.when(dom >= bunches - 8)
    def _():
        add_past_turns(hist, coef_ref, rows, (dom - (bunches - 8)) * 8)

    for ph in range(8):
        halo_ref[ph] = rows[pl.ds(ph, 8, stride=8), :].astype(BF16)


def moment_kernel(scale, coords_ref, index_ref, hist_hbm, coef_hbm, out_ref, hist, coef_ref, rows, sems):
    dom = lax.axis_index(DOM)
    bunches = index_ref.shape[0]
    copy_hist = pltpu.make_async_copy(hist_hbm.at[dom], hist, sems.at[0])
    copy_coef = pltpu.make_async_copy(coef_hbm, coef_ref, sems.at[1])
    copy_hist.start()
    copy_coef.start()
    ids = lane_ids(index_ref.shape[1])

    def one(b, _):
        rows[pl.ds(pl.multiple_of(8 * b, 8), 8), :] = scale * bunch_moment(coords_ref, index_ref, b, ids)
        return 0

    lax.fori_loop(0, bunches, one, 0, unroll=8)
    copy_hist.wait()
    copy_coef.wait()
    add_past_turns(hist, coef_ref, rows, dom * 8)
    blank = jnp.zeros((8, LANES), F32)
    for ph in range(8):
        for half in range(2):
            own = [rows[pl.ds((half * 32 + tile * 8) * 8 + ph, 8, stride=8), :] for tile in range(4)]
            out_ref[ph * 2 + half] = jnp.concatenate([blank, *own, blank], 0).astype(BF16)


def sum_kernel(in_ref, out_ref):
    total = in_ref[0].astype(F32)
    for part in range(1, in_ref.shape[0]):
        total = total + in_ref[part].astype(F32)
    for copy in range(out_ref.shape[0]):
        out_ref[copy] = total[0:40]


def source_kernel(in_ref, out_ref):
    total = in_ref[0]
    for part in range(1, in_ref.shape[0]):
        total = total + in_ref[part]
    total = jnp.concatenate([total, jnp.zeros((8, LANES), F32)], 0).astype(BF16)
    for copy in range(out_ref.shape[0]):
        out_ref[copy] = total


def kick_kernel(total_bunches, in_ref, panels_ref, fill_ref, out_ref, source, bucket):
    bunches = 64
    first = lax.axis_index("bunch") * bunches
    sub = lax.broadcasted_iota(jnp.int32, (8, LANES), 0)
    for tile in range(9):
        column = jnp.zeros((8, LANES), jnp.int32)
        for row in range(8):
            place = first - 8 + tile * 8 + row + total_bunches
            place = jnp.where(place >= total_bunches, place - total_bunches, place)
            column = jnp.where(sub == row, fill_ref[place], column)
        bucket[pl.ds(tile * 8, 8), :] = column
    for ph in range(8):
        source[ph, pl.ds(0, 40), :] = in_ref[2 * ph].astype(F32)[0:40]
        source[ph, pl.ds(40, 32), :] = in_ref[2 * ph + 1].astype(F32)[8:40]
    cycle = 2 * total_bunches
    here = bucket[pl.ds(8, bunches), :]
    gaps = [None] + [(here - bucket[pl.ds(8 - d, bunches), :]) & (cycle - 1) for d in (1, 2, 3)]
    outs = []
    for plane in range(2):
        picked = [[], [], [], []]
        for high in range(4):
            ph = plane * 4 + high
            past = [source[ph, pl.ds(8 - d, bunches), :] for d in range(4)]
            picked[0].append(past[0].astype(BF16))
            for k in (1, 2, 3):
                value = jnp.zeros((bunches, LANES), F32)
                for d in range(1, k + 1):
                    value = jnp.where(gaps[d] == k, past[d], value)
                picked[k].append(value.astype(BF16))
        total = None
        for k in range(4):
            right = jnp.concatenate(picked[k], 1)
            left = panels_ref[plane, k]
            part = lax.dot_general(left, right, (((1,), (1,)), ((), ())), preferred_element_type=F32)
            total = part if total is None else total + part
        outs.append(total)
    kick = jnp.concatenate(outs, 1).astype(BF16)
    for copy in range(out_ref.shape[0]):
        out_ref[copy] = kick


def lookup_kernel(kick_ref, index_ref, out_ref, table):
    bunches = index_ref.shape[0]
    for high in range(4):
        rows = jnp.concatenate([kick_ref[16 * high + part].astype(F32) for part in range(16)], 0)
        table[high] = rows.T
    for block in range(bunches // 8):
        for tile in range(index_ref.shape[1] // LANES):
            index = index_ref[pl.ds(block * 8, 8), pl.ds(tile * LANES, LANES)]
            low = index & (LANES - 1)
            top = index >> 7
            found = []
            for plane in range(2):
                value = None
                for high in range(4):
                    row = table[high, pl.ds(plane * bunches + block * 8, 8), :]
                    got = jnp.take_along_axis(row, low, axis=1)
                    value = got if value is None else jnp.where(top == high, got, value)
                found.append(value)
            out_ref[pl.ds(block * 8, 8), :, pl.ds(tile * LANES, LANES)] = jnp.stack(found, 1).astype(BF16)


def call(kernel, out_shape, in_specs, scratch=()):
    return pl.pallas_call(
        kernel,
        out_shape=out_shape,
        in_specs=in_specs,
        out_specs=VMEM,
        scratch_shapes=list(scratch),
        compiler_params=PARAMS,
    )


def exchange(value, axes):
    return lax.all_to_all(value, axes, 0, 0, tiled=True)


def local(coords, slice_index, history, turn_coef, fill, panels):
    bunches, _, count = coords.shape
    slices = panels.shape[3]
    turns = history.shape[1]
    scale = (slices / (count * lax.axis_size(DOM))) ** 0.5
    shape = jax.ShapeDtypeStruct
    smem = pl.BlockSpec(memory_space=pltpu.SMEM)

    far = pltpu.with_memory_space_constraint
    coef = far(turn_coef.T, pltpu.HBM)
    past = far(history, pltpu.HBM)
    halo = call(
        functools.partial(halo_kernel, scale),
        pltpu.VMEM((8, 8, LANES), BF16),
        [HBM, HBM, HBM, HBM],
        [
            pltpu.VMEM((8, 2, count), BF16),
            pltpu.VMEM((8, count), jnp.int32),
            pltpu.VMEM((turns, 2, slices), F32),
            pltpu.SMEM((2, turns), F32),
            pltpu.VMEM((64, LANES), F32),
            pltpu.SemaphoreType.DMA((4,)),
        ],
    )(far(coords, pltpu.HBM), far(slice_index, pltpu.HBM), past, coef)
    ring = lax.axis_size("bunch")
    halo = lax.ppermute(halo, "bunch", [(i, (i + 1) % ring) for i in range(ring)])
    partial = call(
        functools.partial(moment_kernel, scale),
        shape((16, 48, LANES), BF16),
        [VMEM, VMEM, HBM, HBM],
        [
            pltpu.VMEM((turns, 2, slices), F32),
            pltpu.SMEM((2, turns), F32),
            pltpu.VMEM((bunches * 8, LANES), F32),
            pltpu.SemaphoreType.DMA((2,)),
        ],
    )(coords, slice_index, past, coef)
    partial = partial.reshape(8, 2, 48, LANES).at[:, 0, 0:8].set(halo).reshape(16, 48, LANES)
    part = exchange(partial, ROW16)
    part = call(sum_kernel, shape((4, 40, LANES), F32), [VMEM])(part)
    part = exchange(part, COL4)
    source = call(source_kernel, shape((16, 48, LANES), BF16), [VMEM])(part)
    source = exchange(source, ROW16)
    kick = call(
        functools.partial(kick_kernel, bunches * ring),
        shape((64, 8, LANES), BF16),
        [VMEM, VMEM, smem],
        [pltpu.VMEM((8, 72, LANES), F32), pltpu.VMEM((72, LANES), jnp.int32)],
    )(source, panels, fill)
    kick = exchange(kick, DOM)
    return call(
        lookup_kernel,
        shape((bunches, 2, count), BF16),
        [VMEM, VMEM],
        [pltpu.VMEM((4, LANES, LANES), F32)],
    )(kick, slice_index)


def solution(mesh):
    fine = Mesh(mesh.devices.reshape(8, 4, 2, 8), ("bunch", "zq", "z0", "y"))
    return jax.shard_map(
        local,
        mesh=fine,
        in_specs=(
            P("bunch", None, DOM),
            P("bunch", DOM),
            P("bunch", None, None, None),
            P(),
            P(),
            P(None, None, DOM, None),
        ),
        out_specs=P("bunch", None, DOM),
        check_vma=False,
    )
```

```python
import functools

import jax
import jax.numpy as jnp
from jax import lax
from jax.experimental import pallas as pl
from jax.experimental.pallas import tpu as pltpu
from jax.sharding import Mesh
from jax.sharding import PartitionSpec as P

F32 = jnp.float32
BF16 = jnp.bfloat16
LANES = 128
DOM = ("zq", "z0", "y")
ROW16 = ("z0", "y")
COL4 = ("zq",)
VMEM = pl.BlockSpec(memory_space=pltpu.VMEM)
HBM = pl.BlockSpec(memory_space=pltpu.HBM)
PARAMS = pltpu.CompilerParams(vmem_limit_bytes=32 * 1024 * 1024)


def patterns(count):
    row = lax.broadcasted_iota(jnp.int32, (32, count), 0)
    ids = row.astype(F32).astype(BF16)
    tops = ((row & 3) * 4 + (row >> 3)).astype(F32).astype(BF16)
    return ids, tops, (row & 4) == 0


def four_moments(scale, coords_ref, index_ref, first, consts, rows, start):
    count = index_ref.shape[1]
    ids, tops, lower = consts
    one, none = jnp.ones((), BF16), jnp.zeros((), BF16)
    lefts, rights = [], []
    for b in range(4):
        index = index_ref[pl.ds(first + b, 1), :]
        low = jnp.broadcast_to((index & 31).astype(F32).astype(BF16), (32, count))
        top = jnp.broadcast_to((index >> 5).astype(F32).astype(BF16), (32, count))
        planes = coords_ref[first + b].astype(F32)
        near = jnp.broadcast_to(planes[0:1], (32, count))
        far = jnp.broadcast_to(planes[1:2], (32, count))
        both = jnp.where(lower, near, far).astype(BF16)
        rights.append(jnp.where(low == ids, one, none))
        lefts.append(jnp.where(top == tops, both, none))
    product = lax.dot_general(
        jnp.concatenate(lefts, 0),
        jnp.concatenate(rights, 0),
        (((1,), (1,)), ((), ())),
        preferred_element_type=F32,
    )
    block = lax.broadcasted_iota(jnp.int32, (8, LANES), 1) >> 5
    for b in range(4):
        total = None
        for j in range(4):
            part = product[b * 32 + j * 8 : b * 32 + j * 8 + 8]
            if j != b:
                part = pltpu.roll(part, 32 * ((j - b) % 4), 1)
            total = part if total is None else jnp.where(block == j, part, total)
        rows[pl.ds(pl.multiple_of(start + 8 * b, 8), 8), :] = scale * total


def add_past_turns(hist, coef_ref, rows, first):
    plane_ids = lax.broadcasted_iota(jnp.int32, hist.shape[1:], 0)
    total = jnp.zeros(hist.shape[1:], F32)
    for turn in range(hist.shape[0]):
        total = total + hist[turn] * jnp.where(plane_ids == 0, coef_ref[0, turn], coef_ref[1, turn])
    parts = [
        total[plane : plane + 1, high * LANES : (high + 1) * LANES]
        for plane in range(2)
        for high in range(4)
    ]
    at = pl.ds(pl.multiple_of(first, 8), 8)
    rows[at, :] = rows[at, :] + jnp.concatenate(parts, 0)


def halo_kernel(
    scale, coords_hbm, index_hbm, hist_hbm, coef_hbm, halo_ref, coords, index, hist, coef_ref, rows, sems
):
    dom = lax.axis_index(DOM)
    bunches = index_hbm.shape[0]
    last = pl.ds(bunches - 8, 8)
    copy_index = pltpu.make_async_copy(index_hbm.at[last], index, sems.at[0])
    copy_coords = pltpu.make_async_copy(coords_hbm.at[last], coords, sems.at[1])
    copy_hist = pltpu.make_async_copy(hist_hbm.at[dom], hist, sems.at[2])
    copy_coef = pltpu.make_async_copy(coef_hbm, coef_ref, sems.at[3])
    copy_index.start()
    copy_coords.start()
    copy_hist.start()
    copy_coef.start()
    copy_index.wait()
    copy_coords.wait()
    consts = patterns(index.shape[1])
    for first in (0, 4):
        four_moments(scale, coords, index, first, consts, rows, 8 * first)
    copy_hist.wait()
    copy_coef.wait()

    @pl.when(dom >= bunches - 8)
    def _():
        add_past_turns(hist, coef_ref, rows, (dom - (bunches - 8)) * 8)

    for ph in range(8):
        halo_ref[ph] = rows[pl.ds(ph, 8, stride=8), :].astype(BF16)


def moment_kernel(scale, coords_ref, index_ref, hist_hbm, coef_hbm, out_ref, hist, coef_ref, rows, sems):
    dom = lax.axis_index(DOM)
    bunches = index_ref.shape[0]
    copy_hist = pltpu.make_async_copy(hist_hbm.at[dom], hist, sems.at[0])
    copy_coef = pltpu.make_async_copy(coef_hbm, coef_ref, sems.at[1])
    copy_hist.start()
    copy_coef.start()
    consts = patterns(index_ref.shape[1])

    def some(group, _):
        four_moments(scale, coords_ref, index_ref, 4 * group, consts, rows, 32 * group)
        return 0

    lax.fori_loop(0, bunches // 4, some, 0, unroll=4)
    copy_hist.wait()
    copy_coef.wait()
    add_past_turns(hist, coef_ref, rows, dom * 8)
    blank = jnp.zeros((8, LANES), F32)
    for ph in range(8):
        for half in range(2):
            own = [rows[pl.ds((half * 32 + tile * 8) * 8 + ph, 8, stride=8), :] for tile in range(4)]
            out_ref[ph * 2 + half] = jnp.concatenate([blank, *own, blank], 0).astype(BF16)


def sum_kernel(in_ref, out_ref):
    total = in_ref[0].astype(F32)
    for part in range(1, in_ref.shape[0]):
        total = total + in_ref[part].astype(F32)
    for copy in range(out_ref.shape[0]):
        out_ref[copy] = total[0:40]


def source_kernel(in_ref, out_ref):
    total = in_ref[0]
    for part in range(1, in_ref.shape[0]):
        total = total + in_ref[part]
    total = jnp.concatenate([total, jnp.zeros((8, LANES), F32)], 0).astype(BF16)
    for copy in range(out_ref.shape[0]):
        out_ref[copy] = total


def kick_kernel(total_bunches, in_ref, panels_ref, fill_ref, out_ref, source, bucket):
    bunches = 64
    first = lax.axis_index("bunch") * bunches
    sub = lax.broadcasted_iota(jnp.int32, (8, LANES), 0)
    for tile in range(9):
        column = jnp.zeros((8, LANES), jnp.int32)
        for row in range(8):
            place = first - 8 + tile * 8 + row + total_bunches
            place = jnp.where(place >= total_bunches, place - total_bunches, place)
            column = jnp.where(sub == row, fill_ref[place], column)
        bucket[pl.ds(tile * 8, 8), :] = column
    for ph in range(8):
        source[ph, pl.ds(0, 40), :] = in_ref[2 * ph].astype(F32)[0:40]
        source[ph, pl.ds(40, 32), :] = in_ref[2 * ph + 1].astype(F32)[8:40]
    cycle = 2 * total_bunches
    here = bucket[pl.ds(8, bunches), :]
    gaps = [None] + [(here - bucket[pl.ds(8 - d, bunches), :]) & (cycle - 1) for d in (1, 2, 3)]
    outs = []
    for plane in range(2):
        picked = [[], [], [], []]
        for high in range(4):
            ph = plane * 4 + high
            past = [source[ph, pl.ds(8 - d, bunches), :] for d in range(4)]
            picked[0].append(past[0].astype(BF16))
            for k in (1, 2, 3):
                value = jnp.zeros((bunches, LANES), F32)
                for d in range(1, k + 1):
                    value = jnp.where(gaps[d] == k, past[d], value)
                picked[k].append(value.astype(BF16))
        total = None
        for k in range(4):
            right = jnp.concatenate(picked[k], 1)
            left = panels_ref[plane, k]
            part = lax.dot_general(left, right, (((1,), (1,)), ((), ())), preferred_element_type=F32)
            total = part if total is None else total + part
        outs.append(total)
    kick = jnp.concatenate(outs, 1).astype(BF16)
    for copy in range(out_ref.shape[0]):
        out_ref[copy] = kick


def lookup_kernel(kick_ref, index_ref, out_ref, table):
    bunches = index_ref.shape[0]
    for high in range(4):
        rows = jnp.concatenate([kick_ref[16 * high + part].astype(F32) for part in range(16)], 0)
        table[high] = rows.T
    for block in range(bunches // 8):
        for tile in range(index_ref.shape[1] // LANES):
            index = index_ref[pl.ds(block * 8, 8), pl.ds(tile * LANES, LANES)]
            low = index & (LANES - 1)
            top = index >> 7
            found = []
            for plane in range(2):
                value = None
                for high in range(4):
                    row = table[high, pl.ds(plane * bunches + block * 8, 8), :]
                    got = jnp.take_along_axis(row, low, axis=1)
                    value = got if value is None else jnp.where(top == high, got, value)
                found.append(value)
            out_ref[pl.ds(block * 8, 8), :, pl.ds(tile * LANES, LANES)] = jnp.stack(found, 1).astype(BF16)


def call(kernel, out_shape, in_specs, scratch=()):
    return pl.pallas_call(
        kernel,
        out_shape=out_shape,
        in_specs=in_specs,
        out_specs=VMEM,
        scratch_shapes=list(scratch),
        compiler_params=PARAMS,
    )


def exchange(value, axes):
    return lax.all_to_all(value, axes, 0, 0, tiled=True)


def local(coords, slice_index, history, turn_coef, fill, panels):
    bunches, _, count = coords.shape
    slices = panels.shape[3]
    turns = history.shape[1]
    scale = (slices / (count * lax.axis_size(DOM))) ** 0.5
    shape = jax.ShapeDtypeStruct
    smem = pl.BlockSpec(memory_space=pltpu.SMEM)

    far = pltpu.with_memory_space_constraint
    coef = far(turn_coef.T, pltpu.HBM)
    past = far(history, pltpu.HBM)
    halo = call(
        functools.partial(halo_kernel, scale),
        pltpu.VMEM((8, 8, LANES), BF16),
        [HBM, HBM, HBM, HBM],
        [
            pltpu.VMEM((8, 2, count), BF16),
            pltpu.VMEM((8, count), jnp.int32),
            pltpu.VMEM((turns, 2, slices), F32),
            pltpu.SMEM((2, turns), F32),
            pltpu.VMEM((64, LANES), F32),
            pltpu.SemaphoreType.DMA((4,)),
        ],
    )(far(coords, pltpu.HBM), far(slice_index, pltpu.HBM), past, coef)
    ring = lax.axis_size("bunch")
    halo = lax.ppermute(halo, "bunch", [(i, (i + 1) % ring) for i in range(ring)])
    partial = call(
        functools.partial(moment_kernel, scale),
        shape((16, 48, LANES), BF16),
        [VMEM, VMEM, HBM, HBM],
        [
            pltpu.VMEM((turns, 2, slices), F32),
            pltpu.SMEM((2, turns), F32),
            pltpu.VMEM((bunches * 8, LANES), F32),
            pltpu.SemaphoreType.DMA((2,)),
        ],
    )(coords, slice_index, past, coef)
    partial = partial.reshape(8, 2, 48, LANES).at[:, 0, 0:8].set(halo).reshape(16, 48, LANES)
    part = exchange(partial, ROW16)
    part = call(sum_kernel, shape((4, 40, LANES), F32), [VMEM])(part)
    part = exchange(part, COL4)
    source = call(source_kernel, shape((16, 48, LANES), BF16), [VMEM])(part)
    source = exchange(source, ROW16)
    kick = call(
        functools.partial(kick_kernel, bunches * ring),
        shape((64, 8, LANES), BF16),
        [VMEM, VMEM, smem],
        [pltpu.VMEM((8, 72, LANES), F32), pltpu.VMEM((72, LANES), jnp.int32)],
    )(source, panels, fill)
    kick = exchange(kick, DOM)
    return call(
        lookup_kernel,
        shape((bunches, 2, count), BF16),
        [VMEM, VMEM],
        [pltpu.VMEM((4, LANES, LANES), F32)],
    )(kick, slice_index)


def solution(mesh):
    fine = Mesh(mesh.devices.reshape(8, 4, 2, 8), ("bunch", "zq", "z0", "y"))
    return jax.shard_map(
        local,
        mesh=fine,
        in_specs=(
            P("bunch", None, DOM),
            P("bunch", DOM),
            P("bunch", None, None, None),
            P(),
            P(),
            P(None, None, DOM, None),
        ),
        out_specs=P("bunch", None, DOM),
        check_vma=False,
    )
```

```python
import functools

import jax
import jax.numpy as jnp
from jax import lax
from jax.experimental import pallas as pl
from jax.experimental.pallas import tpu as pltpu
from jax.sharding import Mesh
from jax.sharding import PartitionSpec as P

F32 = jnp.float32
BF16 = jnp.bfloat16
LANES = 128
DOM = ("zq", "z0", "y")
ROW16 = ("z0", "y")
COL4 = ("zq",)
ROW8 = ("y",)
VMEM = pl.BlockSpec(memory_space=pltpu.VMEM)
HBM = pl.BlockSpec(memory_space=pltpu.HBM)
PARAMS = pltpu.CompilerParams(vmem_limit_bytes=32 * 1024 * 1024)


def patterns(count):
    row = lax.broadcasted_iota(jnp.int32, (32, count), 0)
    ids = row.astype(F32).astype(BF16)
    tops = ((row & 3) * 4 + (row >> 3)).astype(F32).astype(BF16)
    return ids, tops, (row & 4) == 0


def four_moments(scale, coords_ref, index_ref, first, consts, rows, start):
    count = index_ref.shape[1]
    ids, tops, lower = consts
    one, none = jnp.ones((), BF16), jnp.zeros((), BF16)
    lefts, rights = [], []
    for b in range(4):
        index = index_ref[pl.ds(first + b, 1), :]
        low = jnp.broadcast_to((index & 31).astype(F32).astype(BF16), (32, count))
        top = jnp.broadcast_to((index >> 5).astype(F32).astype(BF16), (32, count))
        planes = coords_ref[first + b].astype(F32)
        near = jnp.broadcast_to(planes[0:1], (32, count))
        far = jnp.broadcast_to(planes[1:2], (32, count))
        both = jnp.where(lower, near, far).astype(BF16)
        rights.append(jnp.where(low == ids, one, none))
        lefts.append(jnp.where(top == tops, both, none))
    product = lax.dot_general(
        jnp.concatenate(lefts, 0),
        jnp.concatenate(rights, 0),
        (((1,), (1,)), ((), ())),
        preferred_element_type=F32,
    )
    block = lax.broadcasted_iota(jnp.int32, (8, LANES), 1) >> 5
    for b in range(4):
        total = None
        for j in range(4):
            part = product[b * 32 + j * 8 : b * 32 + j * 8 + 8]
            if j != b:
                part = pltpu.roll(part, 32 * ((j - b) % 4), 1)
            total = part if total is None else jnp.where(block == j, part, total)
        rows[pl.ds(pl.multiple_of(start + 8 * b, 8), 8), :] = scale * total


def add_past_turns(hist, coef_ref, rows, first):
    plane_ids = lax.broadcasted_iota(jnp.int32, hist.shape[1:], 0)
    total = jnp.zeros(hist.shape[1:], F32)
    for turn in range(hist.shape[0]):
        total = total + hist[turn] * jnp.where(plane_ids == 0, coef_ref[0, turn], coef_ref[1, turn])
    parts = [
        total[plane : plane + 1, high * LANES : (high + 1) * LANES]
        for plane in range(2)
        for high in range(4)
    ]
    at = pl.ds(pl.multiple_of(first, 8), 8)
    rows[at, :] = rows[at, :] + jnp.concatenate(parts, 0)


def halo_kernel(
    scale, coords_hbm, index_hbm, hist_hbm, coef_hbm, halo_ref, coords, index, hist, coef_ref, rows, sems
):
    dom = lax.axis_index(DOM)
    bunches = index_hbm.shape[0]
    last = pl.ds(bunches - 8, 8)
    copy_index = pltpu.make_async_copy(index_hbm.at[last], index, sems.at[0])
    copy_coords = pltpu.make_async_copy(coords_hbm.at[last], coords, sems.at[1])
    copy_hist = pltpu.make_async_copy(hist_hbm.at[dom], hist, sems.at[2])
    copy_coef = pltpu.make_async_copy(coef_hbm, coef_ref, sems.at[3])
    copy_index.start()
    copy_coords.start()
    copy_hist.start()
    copy_coef.start()
    copy_index.wait()
    copy_coords.wait()
    consts = patterns(index.shape[1])
    for first in (0, 4):
        four_moments(scale, coords, index, first, consts, rows, 8 * first)
    copy_hist.wait()
    copy_coef.wait()

    @pl.when(dom >= bunches - 8)
    def _():
        add_past_turns(hist, coef_ref, rows, (dom - (bunches - 8)) * 8)

    for ph in range(8):
        halo_ref[ph] = rows[pl.ds(ph, 8, stride=8), :].astype(BF16)


def moment_kernel(scale, coords_ref, index_ref, hist_hbm, coef_hbm, out_ref, hist, coef_ref, rows, sems):
    dom = lax.axis_index(DOM)
    bunches = index_ref.shape[0]
    copy_hist = pltpu.make_async_copy(hist_hbm.at[dom], hist, sems.at[0])
    copy_coef = pltpu.make_async_copy(coef_hbm, coef_ref, sems.at[1])
    copy_hist.start()
    copy_coef.start()
    consts = patterns(index_ref.shape[1])

    def some(group, _):
        four_moments(scale, coords_ref, index_ref, 4 * group, consts, rows, 32 * group)
        return 0

    lax.fori_loop(0, bunches // 4, some, 0, unroll=4)
    copy_hist.wait()
    copy_coef.wait()
    add_past_turns(hist, coef_ref, rows, dom * 8)
    blank = jnp.zeros((8, LANES), F32)
    for ph in range(8):
        for half in range(2):
            own = [rows[pl.ds((half * 32 + tile * 8) * 8 + ph, 8, stride=8), :] for tile in range(4)]
            out_ref[ph * 2 + half] = jnp.concatenate([blank, *own, blank], 0).astype(BF16)


def sum_kernel(in_ref, out_ref):
    total = in_ref[0].astype(F32)
    for part in range(1, in_ref.shape[0]):
        total = total + in_ref[part].astype(F32)
    for copy in range(out_ref.shape[0]):
        out_ref[copy] = total[0:40]


def source_kernel(in_ref, out_ref):
    total = in_ref[0]
    for part in range(1, in_ref.shape[0]):
        total = total + in_ref[part]
    total = jnp.concatenate([total, jnp.zeros((8, LANES), F32)], 0).astype(BF16)
    for copy in range(out_ref.shape[0]):
        out_ref[copy] = total


def kick_kernel(total_bunches, in_ref, mine_ref, got_ref, fill_ref, out_ref, source, bucket):
    plane = lax.axis_index("z0")
    bunches = 64
    first = lax.axis_index("bunch") * bunches
    sub = lax.broadcasted_iota(jnp.int32, (8, LANES), 0)
    for tile in range(9):
        column = jnp.zeros((8, LANES), jnp.int32)
        for row in range(8):
            place = first - 8 + tile * 8 + row + total_bunches
            place = jnp.where(place >= total_bunches, place - total_bunches, place)
            column = jnp.where(sub == row, fill_ref[place], column)
        bucket[pl.ds(tile * 8, 8), :] = column
    for high in range(4):
        source[high, pl.ds(0, 40), :] = in_ref[2 * high].astype(F32)[0:40]
        source[high, pl.ds(40, 32), :] = in_ref[2 * high + 1].astype(F32)[8:40]
    cycle = 2 * total_bunches
    here = bucket[pl.ds(8, bunches), :]
    gaps = [None] + [(here - bucket[pl.ds(8 - d, bunches), :]) & (cycle - 1) for d in (1, 2, 3)]
    picked = [[], [], [], []]
    for high in range(4):
        past = [source[high, pl.ds(8 - d, bunches), :] for d in range(4)]
        picked[0].append(past[0].astype(BF16))
        for k in (1, 2, 3):
            value = jnp.zeros((bunches, LANES), F32)
            for d in range(1, k + 1):
                value = jnp.where(gaps[d] == k, past[d], value)
            picked[k].append(value.astype(BF16))
    outs = []
    for panels_ref in (mine_ref, got_ref):
        total = None
        for k in range(4):
            right = jnp.concatenate(picked[k], 1)
            part = lax.dot_general(
                panels_ref[plane, k], right, (((1,), (1,)), ((), ())), preferred_element_type=F32
            )
            total = part if total is None else total + part
        outs.append(total)
    kick = jnp.where(plane == 0, jnp.concatenate(outs, 1), jnp.concatenate(outs[::-1], 1)).astype(BF16)
    for copy in range(out_ref.shape[0]):
        out_ref[copy] = kick


def lookup_kernel(kick_ref, index_ref, out_ref, table):
    bunches = index_ref.shape[0]
    half = LANES // 2
    lower = lax.broadcasted_iota(jnp.int32, (half, LANES), 1) < half
    for high in range(4):
        rows = jnp.concatenate([kick_ref[16 * high + part].astype(F32) for part in range(16)], 0)
        turned = rows.T
        first, second = turned[0:half], turned[half:]
        table[high, pl.ds(0, half), :] = jnp.where(lower, first, pltpu.roll(second, half, 1))
        table[high, pl.ds(half, half), :] = jnp.where(lower, pltpu.roll(first, half, 1), second)
    for block in range(bunches // 8):
        for tile in range(index_ref.shape[1] // LANES):
            index = index_ref[pl.ds(block * 8, 8), pl.ds(tile * LANES, LANES)]
            low = index & (LANES - 1)
            top = index >> 7
            found = []
            for plane in range(2):
                value = None
                for high in range(4):
                    row = table[high, pl.ds(plane * bunches + block * 8, 8), :]
                    got = jnp.take_along_axis(row, low, axis=1)
                    value = got if value is None else jnp.where(top == high, got, value)
                found.append(value)
            out_ref[pl.ds(block * 8, 8), :, pl.ds(tile * LANES, LANES)] = jnp.stack(found, 1).astype(BF16)


def call(kernel, out_shape, in_specs, scratch=()):
    return pl.pallas_call(
        kernel,
        out_shape=out_shape,
        in_specs=in_specs,
        out_specs=VMEM,
        scratch_shapes=list(scratch),
        compiler_params=PARAMS,
    )


def exchange(value, axes):
    return lax.all_to_all(value, axes, 0, 0, tiled=True)


def local(coords, slice_index, history, turn_coef, fill, panels):
    bunches, _, count = coords.shape
    slices = panels.shape[3]
    turns = history.shape[1]
    scale = (slices / (count * lax.axis_size(DOM))) ** 0.5
    shape = jax.ShapeDtypeStruct
    smem = pl.BlockSpec(memory_space=pltpu.SMEM)

    far = pltpu.with_memory_space_constraint
    coef = far(turn_coef.T, pltpu.HBM)
    past = far(history, pltpu.HBM)
    halo = call(
        functools.partial(halo_kernel, scale),
        pltpu.VMEM((8, 8, LANES), BF16),
        [HBM, HBM, HBM, HBM],
        [
            pltpu.VMEM((8, 2, count), BF16),
            pltpu.VMEM((8, count), jnp.int32),
            pltpu.VMEM((turns, 2, slices), F32),
            pltpu.SMEM((2, turns), F32),
            pltpu.VMEM((64, LANES), F32),
            pltpu.SemaphoreType.DMA((4,)),
        ],
    )(far(coords, pltpu.HBM), far(slice_index, pltpu.HBM), past, coef)
    ring = lax.axis_size("bunch")
    halo = lax.ppermute(halo, "bunch", [(i, (i + 1) % ring) for i in range(ring)])
    got = lax.ppermute(panels, "z0", [(0, 1), (1, 0)])
    partial = call(
        functools.partial(moment_kernel, scale),
        shape((16, 48, LANES), BF16),
        [VMEM, VMEM, HBM, HBM],
        [
            pltpu.VMEM((turns, 2, slices), F32),
            pltpu.SMEM((2, turns), F32),
            pltpu.VMEM((bunches * 8, LANES), F32),
            pltpu.SemaphoreType.DMA((2,)),
        ],
    )(coords, slice_index, past, coef)
    partial = partial.reshape(8, 2, 48, LANES).at[:, 0, 0:8].set(halo).reshape(16, 48, LANES)
    part = exchange(partial, ROW16)
    part, got = lax.optimization_barrier((part, got))
    part = call(sum_kernel, shape((4, 40, LANES), F32), [VMEM])(part)
    part = exchange(part, COL4)
    source = call(source_kernel, shape((8, 48, LANES), BF16), [VMEM])(part)
    source = exchange(source, ROW8)
    kick = call(
        functools.partial(kick_kernel, bunches * ring),
        shape((64, 8, LANES), BF16),
        [VMEM, VMEM, VMEM, smem],
        [pltpu.VMEM((4, 72, LANES), F32), pltpu.VMEM((72, LANES), jnp.int32)],
    )(source, panels, got, fill)
    kick = exchange(kick, DOM)
    return call(
        lookup_kernel,
        shape((bunches, 2, count), BF16),
        [VMEM, VMEM],
        [pltpu.VMEM((4, LANES, LANES), F32)],
    )(kick, slice_index)


def solution(mesh):
    fine = Mesh(mesh.devices.reshape(8, 4, 2, 8), ("bunch", "zq", "z0", "y"))
    return jax.shard_map(
        local,
        mesh=fine,
        in_specs=(
            P("bunch", None, DOM),
            P("bunch", DOM),
            P("bunch", None, None, None),
            P(),
            P(),
            P(None, None, DOM, None),
        ),
        out_specs=P("bunch", None, DOM),
        check_vma=False,
    )
```

```python
import functools

import jax
import jax.numpy as jnp
from jax import lax
from jax.experimental import pallas as pl
from jax.experimental.pallas import tpu as pltpu
from jax.sharding import Mesh
from jax.sharding import PartitionSpec as P

F32 = jnp.float32
BF16 = jnp.bfloat16
LANES = 128
DOM = ("z", "yq", "y0")
ROW16 = ("z", "y0")
COL4 = ("yq",)
VMEM = pl.BlockSpec(memory_space=pltpu.VMEM)
HBM = pl.BlockSpec(memory_space=pltpu.HBM)
PARAMS = pltpu.CompilerParams(vmem_limit_bytes=32 * 1024 * 1024)


def patterns(count):
    row = lax.broadcasted_iota(jnp.int32, (32, count), 0)
    ids = row.astype(F32).astype(BF16)
    tops = ((row & 3) * 4 + (row >> 3)).astype(F32).astype(BF16)
    return ids, tops, (row & 4) == 0


def four_moments(scale, coords_ref, index_ref, first, consts, rows, start):
    count = index_ref.shape[1]
    ids, tops, lower = consts
    one, none = jnp.ones((), BF16), jnp.zeros((), BF16)
    lefts, rights = [], []
    for b in range(4):
        index = index_ref[pl.ds(first + b, 1), :]
        low = jnp.broadcast_to((index & 31).astype(F32).astype(BF16), (32, count))
        top = jnp.broadcast_to((index >> 5).astype(F32).astype(BF16), (32, count))
        planes = coords_ref[first + b].astype(F32)
        near = jnp.broadcast_to(planes[0:1], (32, count))
        far = jnp.broadcast_to(planes[1:2], (32, count))
        both = jnp.where(lower, near, far).astype(BF16)
        rights.append(jnp.where(low == ids, one, none))
        lefts.append(jnp.where(top == tops, both, none))
    product = lax.dot_general(
        jnp.concatenate(lefts, 0),
        jnp.concatenate(rights, 0),
        (((1,), (1,)), ((), ())),
        preferred_element_type=F32,
    )
    block = lax.broadcasted_iota(jnp.int32, (8, LANES), 1) >> 5
    for b in range(4):
        total = None
        for j in range(4):
            part = product[b * 32 + j * 8 : b * 32 + j * 8 + 8]
            if j != b:
                part = pltpu.roll(part, 32 * ((j - b) % 4), 1)
            total = part if total is None else jnp.where(block == j, part, total)
        rows[pl.ds(pl.multiple_of(start + 8 * b, 8), 8), :] = scale * total


def add_past_turns(hist, coef_ref, rows, first):
    plane_ids = lax.broadcasted_iota(jnp.int32, hist.shape[1:], 0)
    total = jnp.zeros(hist.shape[1:], F32)
    for turn in range(hist.shape[0]):
        total = total + hist[turn] * jnp.where(plane_ids == 0, coef_ref[0, turn], coef_ref[1, turn])
    parts = [
        total[plane : plane + 1, high * LANES : (high + 1) * LANES]
        for plane in range(2)
        for high in range(4)
    ]
    at = pl.ds(pl.multiple_of(first, 8), 8)
    rows[at, :] = rows[at, :] + jnp.concatenate(parts, 0)


def halo_kernel(
    scale, coords_hbm, index_hbm, hist_hbm, coef_hbm, halo_ref, coords, index, hist, coef_ref, rows, sems
):
    dom = lax.axis_index(DOM)
    bunches = index_hbm.shape[0]
    last = pl.ds(bunches - 8, 8)
    copy_index = pltpu.make_async_copy(index_hbm.at[last], index, sems.at[0])
    copy_coords = pltpu.make_async_copy(coords_hbm.at[last], coords, sems.at[1])
    copy_hist = pltpu.make_async_copy(hist_hbm.at[dom], hist, sems.at[2])
    copy_coef = pltpu.make_async_copy(coef_hbm, coef_ref, sems.at[3])
    copy_index.start()
    copy_coords.start()
    copy_hist.start()
    copy_coef.start()
    copy_index.wait()
    copy_coords.wait()
    consts = patterns(index.shape[1])
    for first in (0, 4):
        four_moments(scale, coords, index, first, consts, rows, 8 * first)
    copy_hist.wait()
    copy_coef.wait()

    @pl.when(dom >= bunches - 8)
    def _():
        add_past_turns(hist, coef_ref, rows, (dom - (bunches - 8)) * 8)

    for ph in range(8):
        halo_ref[ph] = rows[pl.ds(ph, 8, stride=8), :].astype(BF16)


def moment_kernel(scale, coords_ref, index_ref, hist_hbm, coef_hbm, out_ref, hist, coef_ref, rows, sems):
    dom = lax.axis_index(DOM)
    bunches = index_ref.shape[0]
    copy_hist = pltpu.make_async_copy(hist_hbm.at[dom], hist, sems.at[0])
    copy_coef = pltpu.make_async_copy(coef_hbm, coef_ref, sems.at[1])
    copy_hist.start()
    copy_coef.start()
    consts = patterns(index_ref.shape[1])

    def some(group, _):
        four_moments(scale, coords_ref, index_ref, 4 * group, consts, rows, 32 * group)
        return 0

    lax.fori_loop(0, bunches // 4, some, 0, unroll=4)
    copy_hist.wait()
    copy_coef.wait()
    add_past_turns(hist, coef_ref, rows, dom * 8)
    blank = jnp.zeros((8, LANES), F32)
    for ph in range(8):
        for half in range(2):
            own = [rows[pl.ds((half * 32 + tile * 8) * 8 + ph, 8, stride=8), :] for tile in range(4)]
            out_ref[ph * 2 + half] = jnp.concatenate([blank, *own, blank], 0).astype(BF16)


def sum_kernel(in_ref, out_ref):
    total = in_ref[0].astype(F32)
    for part in range(1, in_ref.shape[0]):
        total = total + in_ref[part].astype(F32)
    for copy in range(out_ref.shape[0]):
        out_ref[copy] = total[0:40]


def source_kernel(in_ref, out_ref):
    total = in_ref[0]
    for part in range(1, in_ref.shape[0]):
        total = total + in_ref[part]
    total = jnp.concatenate([total, jnp.zeros((8, LANES), F32)], 0).astype(BF16)
    for copy in range(out_ref.shape[0]):
        out_ref[copy] = total


def kick_kernel(total_bunches, in_ref, panels_ref, fill_ref, out_ref, source, bucket):
    bunches = 64
    first = lax.axis_index("bunch") * bunches
    sub = lax.broadcasted_iota(jnp.int32, (8, LANES), 0)
    for tile in range(9):
        column = jnp.zeros((8, LANES), jnp.int32)
        for row in range(8):
            place = first - 8 + tile * 8 + row + total_bunches
            place = jnp.where(place >= total_bunches, place - total_bunches, place)
            column = jnp.where(sub == row, fill_ref[place], column)
        bucket[pl.ds(tile * 8, 8), :] = column
    for ph in range(8):
        source[ph, pl.ds(0, 40), :] = in_ref[2 * ph].astype(F32)[0:40]
        source[ph, pl.ds(40, 32), :] = in_ref[2 * ph + 1].astype(F32)[8:40]
    cycle = 2 * total_bunches
    here = bucket[pl.ds(8, bunches), :]
    gaps = [None] + [(here - bucket[pl.ds(8 - d, bunches), :]) & (cycle - 1) for d in (1, 2, 3)]
    outs = []
    for plane in range(2):
        picked = [[], [], [], []]
        for high in range(4):
            ph = plane * 4 + high
            past = [source[ph, pl.ds(8 - d, bunches), :] for d in range(4)]
            picked[0].append(past[0].astype(BF16))
            for k in (1, 2, 3):
                value = jnp.zeros((bunches, LANES), F32)
                for d in range(1, k + 1):
                    value = jnp.where(gaps[d] == k, past[d], value)
                picked[k].append(value.astype(BF16))
        total = None
        for k in range(4):
            right = jnp.concatenate(picked[k], 1)
            left = panels_ref[plane, k]
            part = lax.dot_general(left, right, (((1,), (1,)), ((), ())), preferred_element_type=F32)
            total = part if total is None else total + part
        outs.append(total)
    kick = jnp.concatenate(outs, 1).astype(BF16)
    for copy in range(out_ref.shape[0]):
        out_ref[copy] = kick


def lookup_kernel(kick_ref, index_ref, out_ref, table):
    bunches = index_ref.shape[0]
    for high in range(4):
        rows = jnp.concatenate([kick_ref[16 * high + part].astype(F32) for part in range(16)], 0)
        table[high] = rows.T
    for block in range(bunches // 8):
        for tile in range(index_ref.shape[1] // LANES):
            index = index_ref[pl.ds(block * 8, 8), pl.ds(tile * LANES, LANES)]
            low = index & (LANES - 1)
            top = index >> 7
            found = []
            for plane in range(2):
                value = None
                for high in range(4):
                    row = table[high, pl.ds(plane * bunches + block * 8, 8), :]
                    got = jnp.take_along_axis(row, low, axis=1)
                    value = got if value is None else jnp.where(top == high, got, value)
                found.append(value)
            out_ref[pl.ds(block * 8, 8), :, pl.ds(tile * LANES, LANES)] = jnp.stack(found, 1).astype(BF16)


def call(kernel, out_shape, in_specs, scratch=()):
    return pl.pallas_call(
        kernel,
        out_shape=out_shape,
        in_specs=in_specs,
        out_specs=VMEM,
        scratch_shapes=list(scratch),
        compiler_params=PARAMS,
    )


def exchange(value, axes):
    return lax.all_to_all(value, axes, 0, 0, tiled=True)


def local(coords, slice_index, history, turn_coef, fill, panels):
    bunches, _, count = coords.shape
    slices = panels.shape[3]
    turns = history.shape[1]
    scale = (slices / (count * lax.axis_size(DOM))) ** 0.5
    shape = jax.ShapeDtypeStruct
    smem = pl.BlockSpec(memory_space=pltpu.SMEM)

    far = pltpu.with_memory_space_constraint
    coef = far(turn_coef.T, pltpu.HBM)
    past = far(history, pltpu.HBM)
    halo = call(
        functools.partial(halo_kernel, scale),
        pltpu.VMEM((8, 8, LANES), BF16),
        [HBM, HBM, HBM, HBM],
        [
            pltpu.VMEM((8, 2, count), BF16),
            pltpu.VMEM((8, count), jnp.int32),
            pltpu.VMEM((turns, 2, slices), F32),
            pltpu.SMEM((2, turns), F32),
            pltpu.VMEM((64, LANES), F32),
            pltpu.SemaphoreType.DMA((4,)),
        ],
    )(far(coords, pltpu.HBM), far(slice_index, pltpu.HBM), past, coef)
    ring = lax.axis_size("bunch")
    halo = lax.ppermute(halo, "bunch", [(i, (i + 1) % ring) for i in range(ring)])
    partial = call(
        functools.partial(moment_kernel, scale),
        shape((16, 48, LANES), BF16),
        [VMEM, VMEM, HBM, HBM],
        [
            pltpu.VMEM((turns, 2, slices), F32),
            pltpu.SMEM((2, turns), F32),
            pltpu.VMEM((bunches * 8, LANES), F32),
            pltpu.SemaphoreType.DMA((2,)),
        ],
    )(coords, slice_index, past, coef)
    partial = partial.reshape(8, 2, 48, LANES).at[:, 0, 0:8].set(halo).reshape(16, 48, LANES)
    part = exchange(partial, ROW16)
    part = call(sum_kernel, shape((4, 40, LANES), F32), [VMEM])(part)
    part = exchange(part, COL4)
    source = call(source_kernel, shape((16, 48, LANES), BF16), [VMEM])(part)
    source = exchange(source, ROW16)
    kick = call(
        functools.partial(kick_kernel, bunches * ring),
        shape((64, 8, LANES), BF16),
        [VMEM, VMEM, smem],
        [pltpu.VMEM((8, 72, LANES), F32), pltpu.VMEM((72, LANES), jnp.int32)],
    )(source, panels, fill)
    kick = exchange(kick, DOM)
    return call(
        lookup_kernel,
        shape((bunches, 2, count), BF16),
        [VMEM, VMEM],
        [pltpu.VMEM((4, LANES, LANES), F32)],
    )(kick, slice_index)


def solution(mesh):
    fine = Mesh(mesh.devices.reshape(8, 8, 4, 2), ("bunch", "z", "yq", "y0"))
    return jax.shard_map(
        local,
        mesh=fine,
        in_specs=(
            P("bunch", None, DOM),
            P("bunch", DOM),
            P("bunch", None, None, None),
            P(),
            P(),
            P(None, None, DOM, None),
        ),
        out_specs=P("bunch", None, DOM),
        check_vma=False,
    )
```
